256 devices in a mesh: state: 8 (over z), basis: 32 (over x, y, core).
Axes of the slice: x: 4, y: 4, z: 8, core: 2. Of those that a mesh axis runs over, the one named last changes fastest.
Arguments:
- states: float32 [16, 64, 64000], P('state', 'basis'), may hold values from -40 to 40
- membrane_step: float32 [40, 40], replicated, may hold values from -1 to 1
- cavity_forward: float32 [64, 64], replicated, may hold values from -0.75 to 0.75
- coupling: float32 [64, 40], replicated, may hold values from 0.25 to 1
- membrane_forward: float32 [40, 40], replicated, may hold values from -1 to 1
- cavity_back: float32 [64, 64], replicated, may hold values from -9 to 9
- membrane_back: float32 [40, 40], replicated, may hold values from -1 to 1
Outputs:
- orthonormal: float32 [16, 64, 64000], P('state', 'basis')
The draws below stay inside these ranges and needn't reach their ends.
All inputs are finite; a program needn't handle non-finite values.
Results may differ from the reference program's by a relative error of at most 0.000075.
Values sent between devices are 32-bit elements; how exact they have to be, the bound alone decides.
No kernel may reach another device: no remote copies, remote signals or barrier semaphores. Data moves between devices by JAX's collectives and lax.ppermute only.
A program may use at most 192 MiB of HBM per device.

```python
import math
import jax
import jax.numpy as jnp
from jax import lax

C = 64
M = 40
STATES = 16


def draw_states(key, part):
    key_values, key_scale = jax.random.split(key, 2)
    full_shape = (STATES, C, M * M * M)
    scales = 10.0 ** jax.random.uniform(key_scale, (STATES, 1, 1), jnp.float32)
    independent = jax.random.truncated_normal(key_values, -4.0, 4.0, full_shape, jnp.float32)
    return independent * scales


def draw_cavity_back(key, part):
    key_values, key_scale = jax.random.split(key, 2)
    levels = jnp.arange(C, dtype=jnp.float32)[:, None]
    ramped = jnp.sqrt(1.0 + 2.0 * levels / float(C - 1))
    entries = jax.random.truncated_normal(key_values, -4.0, 4.0, (C, C), jnp.float32)
    exponent = jax.random.uniform(key_scale, (C, 1), jnp.float32)
    return entries * float(C) ** (-0.5) * ramped * 10.0 ** exponent


def normal_values(stream_key, shape, spread, most, kind=jnp.bfloat16):
    return jnp.clip(spread * jax.random.normal(stream_key, shape, jnp.float32), -most, most).astype(kind)


def setup_inputs(seed: int = 0) -> dict:
    key_of = jax.random.split(jax.random.key(seed), 8)
    states = draw_states(jax.random.fold_in(key_of[7], 71), 0)
    membrane_step = normal_values(key_of[1], (M, M), M ** -0.5, 1.0, jnp.float32)
    cavity_forward = normal_values(key_of[2], (C, C), C ** -0.5, 0.75, jnp.float32)
    coupling = jnp.clip(jnp.exp(jax.random.uniform(key_of[3], (C, M), jnp.float32, math.log(0.25), math.log(1.0))), 0.25, 1.0)
    membrane_forward = normal_values(key_of[4], (M, M), M ** -0.5, 1.0, jnp.float32)
    cavity_back = draw_cavity_back(jax.random.fold_in(key_of[7], 71), 0)
    membrane_back = normal_values(key_of[6], (M, M), M ** -0.5, 1.0, jnp.float32)
    return {"states": states, "membrane_step": membrane_step, "cavity_forward": cavity_forward, "coupling": coupling, "membrane_forward": membrane_forward, "cavity_back": cavity_back, "membrane_back": membrane_back}


def propagate_state(state, membrane_step, cavity_forward, coupling, membrane_forward, cavity_back, membrane_back):
    joint = M * M * M
    highest = lax.Precision.HIGHEST
    head = jnp.einsum('ab,cbr->car', membrane_step, state.reshape(C, M, joint // M), precision=highest).reshape(C, joint)
    grid = jnp.dot(cavity_forward, head, precision=highest)
    grid = jnp.einsum('qtk,nk->qtn', grid.reshape(C, joint // M, M), membrane_forward, precision=highest)
    weighted = grid * coupling[:, None, :]
    backward = jnp.einsum('qtn,kn->qtk', weighted, membrane_back, precision=highest).reshape(C, joint)
    return jnp.dot(cavity_back, backward, precision=highest)

def reference(states, membrane_step, cavity_forward, coupling, membrane_forward, cavity_back, membrane_back):
    joint = M * M * M
    highest = lax.Precision.HIGHEST

    def single(state):
        return propagate_state(state, membrane_step, cavity_forward, coupling, membrane_forward, cavity_back, membrane_back)
    propagated = lax.map(single, states)
    flattened = propagated.reshape(STATES, C * joint)
    gram = jnp.dot(flattened, flattened.T, precision=highest) / float(C * joint)
    lower_factor = jnp.linalg.cholesky(gram)
    identity = jnp.eye(STATES, dtype=gram.dtype)
    inverse = lax.linalg.triangular_solve(lower_factor, identity, left_side=True, lower=True)
    orthonormal = jnp.dot(inverse, flattened, precision=highest)
    return orthonormal.reshape(STATES, C, joint)
```

```python
import jax
import jax.numpy as jnp
from jax import lax
from jax.experimental import pallas as pl
from jax.experimental.pallas import tpu as pltpu
from jax.sharding import PartitionSpec as P

ROWS = 9
LANES = 128
F32 = jnp.float32
BF16 = jnp.bfloat16
HIGHEST = lax.Precision.HIGHEST
STATES = 16
LEVELS = 64
M = 40
WIDE = 3 * LANES
GROUP = 4
SMALL_VMEM = 24 << 20


def iota(shape, dim):
    return lax.broadcasted_iota(jnp.int32, shape, dim)


def exact_dot(a, b):
    return jnp.dot(a, b, precision=HIGHEST, preferred_element_type=F32)


def split(value):
    high = value.astype(BF16)
    return high, (value - high.astype(F32)).astype(BF16)


def dot3(a, b):
    (ah, al), (bh, bl) = a, b
    out = jnp.dot(ah, bl, preferred_element_type=F32) + jnp.dot(al, bh, preferred_element_type=F32)
    return out + jnp.dot(ah, bh, preferred_element_type=F32)


def head_kernel(states_ref, step_ref, send_ref, x_ref, extra_ref):
    row, col = iota((M, M), 0), iota((M, M), 1)
    order = (col == jnp.where(row < 20, 2 * row, 2 * row - 39)).astype(F32)
    row, col = iota((M, 48), 0), iota((M, 48), 1)
    even = (col < 20) & (row == 2 * col)
    odd = (col >= 24) & (col < 44) & (row == 2 * col - 47)
    step = exact_dot(exact_dot(order, step_ref[...]), (even | odd).astype(F32))

    x_ref[...] = jnp.zeros(x_ref.shape, F32)
    extra_ref[...] = jnp.zeros(extra_ref.shape, F32)
    send_ref[pl.ds(80 * ROWS + 8, 176, stride=ROWS), :] = jnp.zeros((176, LANES), F32)
    lane = iota((M, LANES), 1)
    lane20 = iota((20, LANES), 1)
    for s in range(2):
        for c in range(2):
            e = s * 2 + c

            def tile_in(u):
                return states_ref[pl.ds(s * 1000 + u * 2 + c, 20, stride=50), :]

            for v in range(13):
                x_ref[0:20, v * LANES : (v + 1) * LANES] = tile_in(v)
                low = pltpu.roll(tile_in(12 + v), 64, 1)
                high = pltpu.roll(tile_in(min(13 + v, 24)), 64, 1)
                x_ref[24:44, v * LANES : (v + 1) * LANES] = jnp.where(lane20 < 64, low, high)
            out = exact_dot(step, x_ref[...])
            tiles = [out[:, v * LANES : (v + 1) * LANES] for v in range(13)]

            def chunk(m):
                if m == 0:
                    return tiles[0]
                return jnp.where(
                    lane < 8 * m, pltpu.roll(tiles[m - 1], 8 * m, 1), pltpu.roll(tiles[m], 8 * m, 1)
                )

            last = chunk(12)
            tail = last[32:40]
            extras = [
                pltpu.roll(tiles[12], LANES - 24, 1),
                jnp.concatenate(
                    [
                        tail,
                        pltpu.roll(tail, LANES - 40, 1),
                        pltpu.roll(tail, LANES - 80, 1),
                        jnp.zeros((16, LANES), F32),
                    ],
                    axis=0,
                ),
            ]
            for m in range(12):
                g, h = m // 2, m % 2
                spare = pltpu.roll(extras[g], 120 - 8 * h, 1) if g < 2 else jnp.zeros((M, LANES), F32)
                block = jnp.where(lane < 120, chunk(m), spare)
                send_ref[pl.ds(g * M * ROWS + h * 4 + e, M, stride=ROWS), :] = block
            last = jnp.where(lane < 120, last, 0.0)
            for h in range(2):
                send_ref[pl.ds(240 * ROWS + h * 4 + e, 16, stride=ROWS), :] = last[16 * h : 16 * h + 16]
            inside = (lane >= 32 * e) & (lane < 32 * e + 24)
            for g in range(2):
                moved = pltpu.roll(extras[g], (32 * e - 16) % LANES, 1)
                extra_ref[g] += jnp.where(inside, moved, 0.0)
    for g in range(2):
        send_ref[pl.ds(g * M * ROWS + 8, M, stride=ROWS), :] = extra_ref[g]


def position(shape, dim):
    p = iota(shape, dim)
    h, lane = p >> 7, p & 127
    main = (h < 2) & (lane < 120)
    third = (lane >= 40).astype(jnp.int32) + (lane >= 80).astype(jnp.int32)
    slot = jnp.where(main, 3 * h + third, 6)
    level = jnp.where(main, lane - 40 * third, jnp.where(h < 2, 8 * h + lane - 120, 16 + lane))
    real = (h < 2) | (lane < 24)
    return jnp.where(real, slot, -1), jnp.where(real, level, -1)


def operands_kernel(
    forward_ref, coupling_ref, mem_forward_ref, back_ref, mem_back_ref, cf_ref, cb_ref, mf_ref, mb_ref, w_ref
):
    size = GROUP * LEVELS
    same = (iota((size, size), 0) >> 6) == (iota((size, size), 1) >> 6)
    tall = (iota((size, LEVELS), 1) == (iota((size, LEVELS), 0) & 63)).astype(F32)
    wide = (iota((LEVELS, size), 0) == (iota((LEVELS, size), 1) & 63)).astype(F32)

    def level_of(p):
        return 2 * (p & 31) + ((p >> 5) & 1)

    tall_level = (iota((size, LEVELS), 1) == level_of(iota((size, LEVELS), 0))).astype(F32)
    wide_level = (iota((LEVELS, size), 0) == level_of(iota((LEVELS, size), 1))).astype(F32)
    forward = exact_dot(tall, exact_dot(forward_ref[...], wide_level))
    back = exact_dot(tall_level, exact_dot(back_ref[...], wide))
    for ref, value in ((cf_ref, forward), (cb_ref, back)):
        ref[0], ref[1] = split(jnp.where(same, value, 0.0))

    slot_in, _ = position((WIDE, WIDE), 0)
    slot_out, _ = position((WIDE, WIDE), 1)
    same = (slot_in == slot_out) & (slot_in >= 0)
    _, level = position((WIDE, M), 0)
    down = (level == iota((WIDE, M), 1)).astype(F32)
    _, level = position((M, WIDE), 1)
    across = (level == iota((M, WIDE), 0)).astype(F32)
    for ref, matrix in ((mf_ref, mem_forward_ref), (mb_ref, mem_back_ref)):
        turned = lax.dot_general(
            down, matrix[...], (((1,), (1,)), ((), ())), precision=HIGHEST, preferred_element_type=F32
        )
        ref[0], ref[1] = split(jnp.where(same, exact_dot(turned, across), 0.0))
    w_ref[...] = exact_dot(coupling_ref[...], across)


def step_kernel(recv_ref, cf_ref, cb_ref, mf_ref, mb_ref, w_ref, main_ref, rest_ref, gram_ref, rows_ref):
    lane = iota((32, LANES), 1)
    cf, cb = (cf_ref[0], cf_ref[1]), (cb_ref[0], cb_ref[1])
    mf, mb = (mf_ref[0], mf_ref[1]), (mb_ref[0], mb_ref[1])
    w = jnp.concatenate([w_ref[...]] * GROUP, axis=0)
    size = GROUP * LEVELS
    for group in range(STATES // GROUP):
        parts = []
        for z in range(group * 2, group * 2 + 2):
            seventh = recv_ref[pl.ds(z * 32 * ROWS + 8, 32, stride=ROWS), :]
            for e in range(4):
                halves = [recv_ref[pl.ds(z * 32 * ROWS + h * 4 + e, 32, stride=ROWS), :] for h in range(2)]
                moved = pltpu.roll(seventh, LANES - 32 * e, 1) if e else seventh
                parts.append(jnp.concatenate(halves + [jnp.where(lane < 24, moved, 0.0)], axis=1))
        value = jnp.concatenate(parts, axis=0)
        value = dot3(cf, split(value))
        value = dot3(split(value), mf) * w
        value = dot3(split(value), mb)
        value = dot3(cb, split(value))
        for h in range(2):
            main_ref[h, group * size : (group + 1) * size, :] = value[:, h * LANES : (h + 1) * LANES]
        rest_ref[group * size : (group + 1) * size, :] = value[:, 2 * LANES :]

    for first in range(0, STATES, 4):
        for second in range(0, first + 4, 4):

            def add(tile, sums, first=first, second=second):
                start = pl.multiple_of(tile * 8, 8)
                for load in (
                    lambda st: main_ref[0, pl.ds(st * LEVELS + start, 8), :],
                    lambda st: main_ref[1, pl.ds(st * LEVELS + start, 8), :],
                    lambda st: rest_ref[pl.ds(st * LEVELS + start, 8), :],
                ):
                    a = [load(first + n) for n in range(4)]
                    b = a if first == second else [load(second + n) for n in range(4)]
                    sums = tuple(sums[p * 4 + q] + a[p] * b[q] for p in range(4) for q in range(4))
                return sums

            sums = lax.fori_loop(0, 8, add, (jnp.zeros((8, LANES), F32),) * 16)
            for p in range(4):
                for q in range(4):
                    total = jnp.sum(sums[p * 4 + q], axis=0, keepdims=True)
                    at = (first + p) * STATES + second + q
                    rows_ref[at : at + 1, :] = total
                    if first != second:
                        at = (second + q) * STATES + first + p
                        rows_ref[at : at + 1, :] = total
    flat = lax.dot_general(
        jnp.ones((32, LANES), F32), rows_ref[...], (((1,), (1,)), ((), ())), precision=HIGHEST,
        preferred_element_type=F32,
    )
    for h in range(2):
        gram_ref[pl.ds(h, 32, stride=2), :] = flat[:, h * LANES : (h + 1) * LANES]


def mix_kernel(scale, gram_ref, main_ref, rest_ref, send_ref, coef_ref):
    gram = gram_ref[0:2, :]
    for z in range(1, 8):
        gram = gram + gram_ref[2 * z : 2 * z + 2, :]
    gram = gram * scale
    flat = jnp.concatenate([gram[0:1], gram[1:2]], axis=1)
    row, col = iota((STATES, 2 * LANES), 0), iota((STATES, 2 * LANES), 1)
    spread = jnp.where((col >> 4) == row, flat, 0.0)
    row, col = iota((2 * LANES, LANES), 0), iota((2 * LANES, LANES), 1)
    square = exact_dot(spread, ((row & 15) == col).astype(F32))
    row, col = iota((STATES, LANES), 0), iota((STATES, LANES), 1)
    work = square + (col == row + STATES).astype(F32)
    for j in range(STATES - 1):
        pivot = work[j : j + 1, :]
        factor = work[:, j : j + 1] / work[j : j + 1, j : j + 1]
        work = work - jnp.where(row > j, factor, 0.0) * pivot
    diagonal = jnp.sum(jnp.where(col == row, work, 0.0), axis=1, keepdims=True)
    inverse = work / jnp.sqrt(diagonal)
    row, col = iota((STATES * STATES, STATES), 0), iota((STATES * STATES, STATES), 1)
    repeated = exact_dot(((row >> 4) == col).astype(F32), inverse)
    row, col = iota((STATES * STATES, LANES), 0), iota((STATES * STATES, LANES), 1)
    picked = jnp.where(col == (row & 15) + STATES, repeated, 0.0)
    coef_ref[...] = exact_dot(picked, jnp.ones((LANES, LANES), F32))

    lane = iota((8, LANES), 1)

    def mixed(loads):
        values = [[load(st) for load in loads] for st in range(STATES)]
        for t in range(STATES):
            sums = [None, None]
            for st in range(t + 1):
                factor = coef_ref[t * STATES + st : t * STATES + st + 1, :]
                for n in range(2):
                    term = factor * values[st][n]
                    sums[n] = term if sums[n] is None else sums[n] + term
            yield t, sums

    def tile(n, carry):
        start = pl.multiple_of(n * 8, 8)
        for c in range(2):
            loads = [
                lambda st, h=h: main_ref[h, pl.ds(st * LEVELS + c * 32 + start, 8), :] for h in range(2)
            ]
            for t, sums in mixed(loads):
                z, s = t // 2, t % 2
                for h in range(2):
                    at = (z * 32 + start) * ROWS + h * 4 + s * 2 + c
                    send_ref[pl.ds(at, 8, stride=ROWS), :] = sums[h]
        loads = [lambda st, c=c: rest_ref[pl.ds(st * LEVELS + c * 32 + start, 8), :] for c in range(2)]
        seventh = None
        for t, sums in mixed(loads):
            z, s = t // 2, t % 2
            for c in range(2):
                e = s * 2 + c
                value = pltpu.roll(sums[c], 32 * e, 1) if e else sums[c]
                seventh = value if e == 0 else seventh + value
            if s == 1:
                send_ref[pl.ds((z * 32 + start) * ROWS + 8, 8, stride=ROWS), :] = seventh
        return carry

    lax.fori_loop(0, 4, tile, 0)


def tail_kernel(recv_ref, out_ref, chunk_ref, tile_ref):
    lane = iota((M, LANES), 1)
    lane8 = iota((8, LANES), 1)
    lane20 = iota((20, LANES), 1)
    for s in range(2):
        for c in range(2):
            e = s * 2 + c
            for m in range(12):
                g, h = m // 2, m % 2
                chunk_ref[m] = recv_ref[pl.ds(g * M * ROWS + h * 4 + e, M, stride=ROWS), :]
            for h in range(2):
                chunk_ref[12, 16 * h : 16 * h + 16] = recv_ref[pl.ds(240 * ROWS + h * 4 + e, 16, stride=ROWS), :]
            extras = []
            for g in range(2):
                seventh = recv_ref[pl.ds(g * M * ROWS + 8, M, stride=ROWS), :]
                extra = jnp.where(
                    lane < 8, pltpu.roll(chunk_ref[2 * g], 8, 1), pltpu.roll(chunk_ref[2 * g + 1], 16, 1)
                )
                extras.append(jnp.where(lane < 16, extra, pltpu.roll(seventh, (16 - 32 * e) % LANES, 1)))
            first, second, third = (extras[1][8 * n : 8 * n + 8] for n in range(3))
            chunk_ref[12, 32:40] = jnp.where(
                lane8 < 40,
                first,
                jnp.where(lane8 < 80, pltpu.roll(second, 40, 1), pltpu.roll(third, 80, 1)),
            )
            chunk_ref[13] = extras[0]
            for v in range(13):
                low = pltpu.roll(chunk_ref[v], (LANES - 8 * v) % LANES, 1) if v else chunk_ref[v]
                high = pltpu.roll(chunk_ref[v + 1], 120 - 8 * v, 1)
                tile_ref[v] = jnp.where(lane < 120 - 8 * v, low, high)
            for u in range(25):
                if u < 12:
                    value = tile_ref[u, 0:20]
                else:
                    low = tile_ref[12, 0:20] if u == 12 else pltpu.roll(tile_ref[u - 13, 20:40], 64, 1)
                    high = pltpu.roll(tile_ref[u - 12, 20:40], 64, 1)
                    value = jnp.where(lane20 < 64, low, high)
                out_ref[pl.ds(s * 1000 + u * 2 + c, 20, stride=50), :] = value


def call(kernel, outs, scratch, cost):
    return pl.pallas_call(
        kernel,
        out_shape=outs,
        scratch_shapes=scratch,
        compiler_params=pltpu.CompilerParams(vmem_limit_bytes=SMALL_VMEM),
        cost_estimate=pl.CostEstimate(flops=cost, bytes_accessed=1 << 20, transcendentals=0),
    )


def shape(*dims, dtype=F32):
    return jax.ShapeDtypeStruct(dims, dtype)


def exchange(blocks, axes):
    count = 1
    for a in axes:
        count *= lax.axis_size(a)
    rows = blocks.shape[0] // count
    value = blocks.reshape(count, 1, rows * LANES)
    value = lax.all_to_all(value, axes, split_axis=0, concat_axis=0, tiled=True)
    return value.reshape(blocks.shape)


def body(states, membrane_step, cavity_forward, coupling, membrane_forward, cavity_back, membrane_back):
    panel, levels, joint = states.shape
    everyone = ("state", "basis")
    linear = states.reshape(panel, levels, joint // LANES, LANES)
    linear = jnp.swapaxes(linear, 1, 2).reshape(-1, LANES)
    blocks = shape(256 * ROWS, LANES)
    send = call(
        head_kernel,
        blocks,
        [pltpu.VMEM((48, 13 * LANES), F32), pltpu.VMEM((2, M, LANES), F32)],
        1 << 20,
    )(linear, membrane_step)
    size = GROUP * LEVELS
    cf, cb, mf, mb, w = call(
        operands_kernel,
        (
            shape(2, size, size, dtype=BF16),
            shape(2, size, size, dtype=BF16),
            shape(2, WIDE, WIDE, dtype=BF16),
            shape(2, WIDE, WIDE, dtype=BF16),
            shape(LEVELS, WIDE),
        ),
        [],
        1 << 27,
    )(cavity_forward, coupling, membrane_forward, cavity_back, membrane_back)
    recv = exchange(send, everyone)
    main, rest, gram = call(
        step_kernel,
        (shape(2, STATES * LEVELS, LANES), shape(STATES * LEVELS, LANES), shape(64, LANES)),
        [pltpu.VMEM((STATES * STATES, LANES), F32)],
        1 << 30,
    )(recv, cf, cb, mf, mb, w)
    gram = lax.all_to_all(gram.reshape(32, 2, LANES), "basis", split_axis=0, concat_axis=0, tiled=True)
    gram = jnp.broadcast_to(jnp.sum(gram, axis=0, keepdims=True), (8, 2, LANES))
    gram = lax.all_to_all(gram, "state", split_axis=0, concat_axis=0, tiled=True)
    scale = 1.0 / float(LEVELS * joint)
    send = call(
        lambda *refs: mix_kernel(scale, *refs), blocks, [pltpu.VMEM((STATES * STATES, LANES), F32)], 1 << 27
    )(gram.reshape(16, LANES), main, rest)
    recv = exchange(send, everyone)
    out = call(
        tail_kernel,
        shape(2000, LANES),
        [pltpu.VMEM((14, M, LANES), F32), pltpu.VMEM((13, M, LANES), F32)],
        1 << 20,
    )(recv)
    out = out.reshape(panel, joint // LANES, levels, LANES)
    return jnp.swapaxes(out, 1, 2).reshape(panel, levels, joint)


def solution(mesh):
    in_specs = (P("state", "basis", None), P(), P(), P(), P(), P(), P())
    out_specs = P("state", "basis", None)
    return jax.shard_map(body, mesh=mesh, in_specs=in_specs, out_specs=out_specs, check_vma=False)
```

```python
import jax
import jax.numpy as jnp
from jax import lax
from jax.experimental.layout import Layout, with_layout_constraint
from jax.experimental import pallas as pl
from jax.experimental.pallas import tpu as pltpu
from jax.sharding import PartitionSpec as P

ROWS = 9
LANES = 128
F32 = jnp.float32
BF16 = jnp.bfloat16
HIGHEST = lax.Precision.HIGHEST
STATES = 16
LEVELS = 64
M = 40
GROUP = 4
SMALL_VMEM = 24 << 20
LARGE_VMEM = 60 << 20


def iota(shape, dim):
    return lax.broadcasted_iota(jnp.int32, shape, dim)


def exact_dot(a, b):
    return jnp.dot(a, b, precision=HIGHEST, preferred_element_type=F32)


def split(value):
    high = value.astype(BF16)
    return high, (value - high.astype(F32)).astype(BF16)


def dot3(a, b):
    (ah, al), (bh, bl) = a, b
    out = jnp.dot(ah, bl, preferred_element_type=F32) + jnp.dot(al, bh, preferred_element_type=F32)
    return out + jnp.dot(ah, bh, preferred_element_type=F32)


def head_kernel(states_hbm, step_hbm, send_ref, states_ref, step_ref, x_ref, extra_ref, sems):
    step_copy = pltpu.make_async_copy(step_hbm, step_ref, sems.at[2])
    step_copy.start()
    copies = []
    for s in range(2):
        part = pl.ds(s * 1000, 1000)
        copies.append(pltpu.make_async_copy(states_hbm.at[part], states_ref.at[part], sems.at[s]))
        copies[-1].start()
    x_ref[...] = jnp.zeros(x_ref.shape, F32)
    extra_ref[...] = jnp.zeros(extra_ref.shape, F32)
    send_ref[pl.ds(80 * ROWS + 8, 176, stride=ROWS), :] = jnp.zeros((176, LANES), F32)
    row, col = iota((M, M), 0), iota((M, M), 1)
    order = (col == jnp.where(row < 20, 2 * row, 2 * row - 39)).astype(F32)
    row, col = iota((M, 48), 0), iota((M, 48), 1)
    even = (col < 20) & (row == 2 * col)
    odd = (col >= 24) & (col < 44) & (row == 2 * col - 47)
    step_copy.wait()
    step = exact_dot(exact_dot(order, step_ref[...]), (even | odd).astype(F32))
    lane = iota((M, LANES), 1)
    lane20 = iota((20, LANES), 1)
    for s in range(2):
        copies[s].wait()
        for c in range(2):
            e = s * 2 + c

            def tile_in(u):
                return states_ref[pl.ds(s * 1000 + u * 2 + c, 20, stride=50), :]

            for v in range(13):
                x_ref[0:20, v * LANES : (v + 1) * LANES] = tile_in(v)
                low = pltpu.roll(tile_in(12 + v), 64, 1)
                high = pltpu.roll(tile_in(min(13 + v, 24)), 64, 1)
                x_ref[24:44, v * LANES : (v + 1) * LANES] = jnp.where(lane20 < 64, low, high)
            out = exact_dot(step, x_ref[...])
            tiles = [out[:, v * LANES : (v + 1) * LANES] for v in range(13)]

            def chunk(m):
                if m == 0:
                    return tiles[0]
                return jnp.where(
                    lane < 8 * m, pltpu.roll(tiles[m - 1], 8 * m, 1), pltpu.roll(tiles[m], 8 * m, 1)
                )

            last = chunk(12)
            tail = last[32:40]
            extras = [
                pltpu.roll(tiles[12], LANES - 24, 1),
                jnp.concatenate(
                    [
                        tail,
                        pltpu.roll(tail, LANES - 40, 1),
                        pltpu.roll(tail, LANES - 80, 1),
                        jnp.zeros((16, LANES), F32),
                    ],
                    axis=0,
                ),
            ]
            for m in range(12):
                g, h = m // 2, m % 2
                spare = pltpu.roll(extras[g], 120 - 8 * h, 1) if g < 2 else jnp.zeros((M, LANES), F32)
                block = jnp.where(lane < 120, chunk(m), spare)
                send_ref[pl.ds(g * M * ROWS + h * 4 + e, M, stride=ROWS), :] = block
            last = jnp.where(lane < 120, last, 0.0)
            for h in range(2):
                send_ref[pl.ds(240 * ROWS + h * 4 + e, 16, stride=ROWS), :] = last[16 * h : 16 * h + 16]
            inside = (lane >= 32 * e) & (lane < 32 * e + 24)
            for g in range(2):
                moved = pltpu.roll(extras[g], (32 * e - 16) % LANES, 1)
                extra_ref[g] += jnp.where(inside, moved, 0.0)
    for g in range(2):
        send_ref[pl.ds(g * M * ROWS + 8, M, stride=ROWS), :] = extra_ref[g]


def operands_kernel(
    forward_ref, coupling_ref, mem_forward_ref, back_ref, mem_back_ref,
    cf_ref, cb_ref, mf_ref, mb_ref, ef_ref, eb_ref, w_ref,
):
    size = 2 * LEVELS
    same = (iota((size, size), 0) >> 6) == (iota((size, size), 1) >> 6)
    tall = (iota((size, LEVELS), 1) == (iota((size, LEVELS), 0) & 63)).astype(F32)
    wide = (iota((LEVELS, size), 0) == (iota((LEVELS, size), 1) & 63)).astype(F32)

    def level_of(p):
        return 2 * (p & 31) + ((p >> 5) & 1)

    tall_level = (iota((size, LEVELS), 1) == level_of(iota((size, LEVELS), 0))).astype(F32)
    wide_level = (iota((LEVELS, size), 0) == level_of(iota((LEVELS, size), 1))).astype(F32)
    forward = exact_dot(tall, exact_dot(forward_ref[...], wide_level))
    back = exact_dot(tall_level, exact_dot(back_ref[...], wide))
    for ref, value in ((cf_ref, forward), (cb_ref, back)):
        ref[0], ref[1] = split(jnp.where(same, value, 0.0))

    def threes(lane):
        third = (lane >= 40).astype(jnp.int32) + (lane >= 80).astype(jnp.int32)
        return jnp.where(lane < 120, third, -1), jnp.where(lane < 120, lane - 40 * third, -1)

    def sevenths(lane):
        real = (lane & 63) < 40
        return jnp.where(real, lane >> 6, -1), jnp.where(real, lane & 63, -1)

    for n, (place, fref, bref) in enumerate(((threes, mf_ref, mb_ref), (sevenths, ef_ref, eb_ref))):
        slot_in, _ = place(iota((LANES, LANES), 0))
        slot_out, _ = place(iota((LANES, LANES), 1))
        same = (slot_in == slot_out) & (slot_in >= 0)
        down = (place(iota((LANES, M), 0))[1] == iota((LANES, M), 1)).astype(F32)
        across = (place(iota((M, LANES), 1))[1] == iota((M, LANES), 0)).astype(F32)
        for ref, matrix in ((fref, mem_forward_ref), (bref, mem_back_ref)):
            turned = lax.dot_general(
                down, matrix[...], (((1,), (1,)), ((), ())), precision=HIGHEST, preferred_element_type=F32
            )
            ref[0], ref[1] = split(jnp.where(same, exact_dot(turned, across), 0.0))
        w_ref[n] = exact_dot(coupling_ref[...], across)


def twice(block):
    zero = jnp.zeros_like(block)
    return jnp.concatenate(
        [jnp.concatenate([block, zero], axis=1), jnp.concatenate([zero, block], axis=1)], axis=0
    )


def turn(value, shift):
    shift = shift % LANES
    return pltpu.roll(value, shift, 1) if shift else value


def step_kernel(
    recv_ref, cf_ref, cb_ref, mf_ref, mb_ref, ef_ref, eb_ref, w_ref, main_ref, rest_ref, gram_ref, rows_ref
):
    cf, cb, mf, mb = ((twice(ref[0]), twice(ref[1])) for ref in (cf_ref, cb_ref, mf_ref, mb_ref))
    ef, eb = (ef_ref[0], ef_ref[1]), (eb_ref[0], eb_ref[1])
    w_half = jnp.concatenate([w_ref[0]] * GROUP, axis=0)
    w_main = jnp.concatenate([w_half, w_half], axis=1)
    w_rest = jnp.concatenate([w_ref[1]] * GROUP, axis=0)
    size = GROUP * LEVELS
    groups = STATES // GROUP

    lane = iota((32, LANES), 1)
    parts = []
    for part in range(2):
        sevenths = [recv_ref[pl.ds((2 * g + part) * 32 * ROWS + 8, 32, stride=ROWS), :] for g in range(groups)]
        for e in range(4):
            value = turn(sevenths[3], 32 * (3 - e))
            for g in range(2, -1, -1):
                value = jnp.where(lane < 32 * g + 32, turn(sevenths[g], 32 * (g - e)), value)
            parts.append(jnp.where((lane & 31) < 24, value, 0.0))
    rest = dot3(cf, split(jnp.concatenate(parts, axis=0)))

    lane = iota((size, LANES), 1)
    rest_back = jnp.zeros((size, LANES), F32)
    for pair in range(groups // 2):
        mains = []
        extra = jnp.zeros((size, LANES), F32)
        for half in range(2):
            group = 2 * pair + half
            parts = []
            for z in range(group * 2, group * 2 + 2):
                for e in range(4):
                    tiles = [recv_ref[pl.ds(z * 32 * ROWS + h * 4 + e, 32, stride=ROWS), :] for h in range(2)]
                    parts.append(jnp.concatenate(tiles, axis=1))
            value = dot3(cf, split(jnp.concatenate(parts, axis=0)))
            at = 64 * half
            moved = jnp.where(lane < at + 16, turn(value[:, LANES:], at + 16), turn(rest, at + 16 - 32 * group))
            moved = jnp.where(lane < at + 8, turn(value[:, :LANES], at + 8), moved)
            extra = jnp.where((lane >= at) & (lane < at + 40), moved, extra)
            value = dot3(split(value), mf) * w_main
            mains.append(dot3(split(value), mb))
        extra = dot3(split(extra), ef) * w_rest
        extra = dot3(split(extra), eb)
        for half in range(2):
            group = 2 * pair + half
            at = 64 * half
            tiles = []
            for h in range(2):
                tile = mains[half][:, h * LANES : (h + 1) * LANES]
                tiles.append(jnp.where(lane < 120, tile, turn(extra, 120 - at - 8 * h)))
            value = dot3(cb, split(jnp.concatenate(tiles, axis=1)))
            for h in range(2):
                main_ref[h, group * size : (group + 1) * size, :] = value[:, h * LANES : (h + 1) * LANES]
            inside = (lane >= 32 * group) & (lane < 32 * group + 24)
            rest_back = jnp.where(inside, turn(extra, 32 * group - at - 16), rest_back)
    rest = dot3(cb, split(rest_back))
    for group in range(groups):
        rest_ref[group * size : (group + 1) * size, :] = jnp.where(lane < 24, turn(rest, -32 * group), 0.0)

    for first in range(0, STATES, 4):
        for second in range(0, first + 4, 4):

            def add(tile, sums, first=first, second=second):
                start = pl.multiple_of(tile * 8, 8)
                for load in (
                    lambda st: main_ref[0, pl.ds(st * LEVELS + start, 8), :],
                    lambda st: main_ref[1, pl.ds(st * LEVELS + start, 8), :],
                    lambda st: rest_ref[pl.ds(st * LEVELS + start, 8), :],
                ):
                    a = [load(first + n) for n in range(4)]
                    b = a if first == second else [load(second + n) for n in range(4)]
                    sums = tuple(sums[p * 4 + q] + a[p] * b[q] for p in range(4) for q in range(4))
                return sums

            sums = lax.fori_loop(0, 8, add, (jnp.zeros((8, LANES), F32),) * 16)
            for p in range(4):
                for q in range(4):
                    total = jnp.sum(sums[p * 4 + q], axis=0, keepdims=True)
                    at = (first + p) * STATES + second + q
                    rows_ref[at : at + 1, :] = total
                    if first != second:
                        at = (second + q) * STATES + first + p
                        rows_ref[at : at + 1, :] = total
    flat = lax.dot_general(
        jnp.ones((32, LANES), F32), rows_ref[...], (((1,), (1,)), ((), ())), precision=HIGHEST,
        preferred_element_type=F32,
    )
    for h in range(2):
        gram_ref[pl.ds(h, 32, stride=2), :] = flat[:, h * LANES : (h + 1) * LANES]


def mix_kernel(scale, gram_ref, main_ref, rest_ref, send_ref, coef_ref):
    gram = gram_ref[0:2, :]
    for z in range(1, 8):
        gram = gram + gram_ref[2 * z : 2 * z + 2, :]
    gram = gram * scale
    flat = jnp.concatenate([gram[0:1], gram[1:2]], axis=1)
    row, col = iota((STATES, 2 * LANES), 0), iota((STATES, 2 * LANES), 1)
    spread = jnp.where((col >> 4) == row, flat, 0.0)
    row, col = iota((2 * LANES, LANES), 0), iota((2 * LANES, LANES), 1)
    square = exact_dot(spread, ((row & 15) == col).astype(F32))
    row, col = iota((STATES, LANES), 0), iota((STATES, LANES), 1)
    work = square + (col == row + STATES).astype(F32)
    for j in range(STATES - 1):
        pivot = work[j : j + 1, :]
        factor = work[:, j : j + 1] / work[j : j + 1, j : j + 1]
        work = work - jnp.where(row > j, factor, 0.0) * pivot
    diagonal = jnp.sum(jnp.where(col == row, work, 0.0), axis=1, keepdims=True)
    inverse = work / jnp.sqrt(diagonal)
    row, col = iota((STATES * STATES, STATES), 0), iota((STATES * STATES, STATES), 1)
    repeated = exact_dot(((row >> 4) == col).astype(F32), inverse)
    row, col = iota((STATES * STATES, LANES), 0), iota((STATES * STATES, LANES), 1)
    picked = jnp.where(col == (row & 15) + STATES, repeated, 0.0)
    coef_ref[...] = exact_dot(picked, jnp.ones((LANES, LANES), F32))

    lane = iota((8, LANES), 1)

    def mixed(loads):
        values = [[load(st) for load in loads] for st in range(STATES)]
        for t in range(STATES):
            sums = [None, None]
            for st in range(t + 1):
                factor = coef_ref[t * STATES + st : t * STATES + st + 1, :]
                for n in range(2):
                    term = factor * values[st][n]
                    sums[n] = term if sums[n] is None else sums[n] + term
            yield t, sums

    def tile(n, carry):
        start = pl.multiple_of(n * 8, 8)
        for c in range(2):
            loads = [
                lambda st, h=h: main_ref[h, pl.ds(st * LEVELS + c * 32 + start, 8), :] for h in range(2)
            ]
            for t, sums in mixed(loads):
                z, s = t // 2, t % 2
                for h in range(2):
                    at = (z * 32 + start) * ROWS + h * 4 + s * 2 + c
                    send_ref[pl.ds(at, 8, stride=ROWS), :] = sums[h]
        loads = [lambda st, c=c: rest_ref[pl.ds(st * LEVELS + c * 32 + start, 8), :] for c in range(2)]
        seventh = None
        for t, sums in mixed(loads):
            z, s = t // 2, t % 2
            for c in range(2):
                e = s * 2 + c
                value = pltpu.roll(sums[c], 32 * e, 1) if e else sums[c]
                seventh = value if e == 0 else seventh + value
            if s == 1:
                send_ref[pl.ds((z * 32 + start) * ROWS + 8, 8, stride=ROWS), :] = seventh
        return carry

    lax.fori_loop(0, 4, tile, 0)


def tail_kernel(recv_ref, out_ref, chunk_ref, tile_ref):
    lane = iota((M, LANES), 1)
    lane8 = iota((8, LANES), 1)
    lane20 = iota((20, LANES), 1)
    for s in range(2):
        for c in range(2):
            e = s * 2 + c
            for m in range(12):
                g, h = m // 2, m % 2
                chunk_ref[m] = recv_ref[pl.ds(g * M * ROWS + h * 4 + e, M, stride=ROWS), :]
            for h in range(2):
                chunk_ref[12, 16 * h : 16 * h + 16] = recv_ref[pl.ds(240 * ROWS + h * 4 + e, 16, stride=ROWS), :]
            extras = []
            for g in range(2):
                seventh = recv_ref[pl.ds(g * M * ROWS + 8, M, stride=ROWS), :]
                extra = jnp.where(
                    lane < 8, pltpu.roll(chunk_ref[2 * g], 8, 1), pltpu.roll(chunk_ref[2 * g + 1], 16, 1)
                )
                extras.append(jnp.where(lane < 16, extra, pltpu.roll(seventh, (16 - 32 * e) % LANES, 1)))
            first, second, third = (extras[1][8 * n : 8 * n + 8] for n in range(3))
            chunk_ref[12, 32:40] = jnp.where(
                lane8 < 40,
                first,
                jnp.where(lane8 < 80, pltpu.roll(second, 40, 1), pltpu.roll(third, 80, 1)),
            )
            chunk_ref[13] = extras[0]
            for v in range(13):
                low = pltpu.roll(chunk_ref[v], (LANES - 8 * v) % LANES, 1) if v else chunk_ref[v]
                high = pltpu.roll(chunk_ref[v + 1], 120 - 8 * v, 1)
                tile_ref[v] = jnp.where(lane < 120 - 8 * v, low, high)
            for u in range(25):
                if u < 12:
                    value = tile_ref[u, 0:20]
                else:
                    low = tile_ref[12, 0:20] if u == 12 else pltpu.roll(tile_ref[u - 13, 20:40], 64, 1)
                    high = pltpu.roll(tile_ref[u - 12, 20:40], 64, 1)
                    value = jnp.where(lane20 < 64, low, high)
                out_ref[pl.ds(s * 1000 + u * 2 + c, 20, stride=50), :] = value


def call(kernel, outs, scratch, cost, places="v", limit=SMALL_VMEM):
    spaces = {"v": pltpu.VMEM, "h": pltpu.HBM}
    return pl.pallas_call(
        kernel,
        out_shape=outs,
        in_specs=[pl.BlockSpec(memory_space=spaces[p]) for p in places],
        scratch_shapes=scratch,
        compiler_params=pltpu.CompilerParams(vmem_limit_bytes=limit),
        cost_estimate=pl.CostEstimate(flops=cost, bytes_accessed=1 << 20, transcendentals=0),
    )


def shape(*dims, dtype=F32):
    return jax.ShapeDtypeStruct(dims, dtype)


def exchange(blocks, axes):
    count = 1
    for a in axes:
        count *= lax.axis_size(a)
    rows = blocks.shape[0] // count
    value = blocks.reshape(count, 1, rows * LANES)
    value = lax.all_to_all(value, axes, split_axis=0, concat_axis=0, tiled=True)
    return value.reshape(blocks.shape)


def body(states, membrane_step, cavity_forward, coupling, membrane_forward, cavity_back, membrane_back):
    panel, levels, joint = states.shape
    everyone = ("state", "basis")
    by_tile = Layout(major_to_minor=(0, 2, 1, 3))
    linear = with_layout_constraint(states.reshape(panel, levels, joint // LANES, LANES), by_tile)
    linear = jnp.swapaxes(linear, 1, 2).reshape(-1, LANES)
    blocks = shape(256 * ROWS, LANES)
    send = call(
        head_kernel,
        blocks,
        [
            pltpu.VMEM((2000, LANES), F32),
            pltpu.VMEM((M, M), F32),
            pltpu.VMEM((48, 13 * LANES), F32),
            pltpu.VMEM((2, M, LANES), F32),
            pltpu.SemaphoreType.DMA((3,)),
        ],
        1 << 20,
        "hh",
        LARGE_VMEM,
    )(linear, membrane_step)
    squares = [shape(2, LANES, LANES, dtype=BF16)] * 6
    operands = call(operands_kernel, (*squares, shape(2, LEVELS, LANES)), [], 1 << 27, "vvvvv")(
        cavity_forward, coupling, membrane_forward, cavity_back, membrane_back
    )
    recv = exchange(send, everyone)
    main, rest, gram = call(
        step_kernel,
        (shape(2, STATES * LEVELS, LANES), shape(STATES * LEVELS, LANES), shape(64, LANES)),
        [pltpu.VMEM((STATES * STATES, LANES), F32)],
        1 << 30,
        "vvvvvvvv",
    )(recv, *operands)
    gram = lax.all_to_all(gram.reshape(32, 2, LANES), "basis", split_axis=0, concat_axis=0, tiled=True)
    gram = jnp.broadcast_to(jnp.sum(gram, axis=0, keepdims=True), (8, 2, LANES))
    gram = lax.all_to_all(gram, "state", split_axis=0, concat_axis=0, tiled=True)
    scale = 1.0 / float(LEVELS * joint)
    send = call(
        lambda *refs: mix_kernel(scale, *refs),
        blocks,
        [pltpu.VMEM((STATES * STATES, LANES), F32)],
        1 << 27,
        "vvv",
    )(gram.reshape(16, LANES), main, rest)
    recv = exchange(send, everyone)
    out = call(
        tail_kernel,
        shape(2000, LANES),
        [pltpu.VMEM((14, M, LANES), F32), pltpu.VMEM((13, M, LANES), F32)],
        1 << 20,
    )(recv)
    out = out.reshape(panel, joint // LANES, levels, LANES)
    return with_layout_constraint(jnp.swapaxes(out, 1, 2), by_tile).reshape(panel, levels, joint)


def solution(mesh):
    in_specs = (P("state", "basis", None), P(), P(), P(), P(), P(), P())
    out_specs = P("state", "basis", None)
    return jax.shard_map(body, mesh=mesh, in_specs=in_specs, out_specs=out_specs, check_vma=False)
```

```python
import jax
import jax.numpy as jnp
from jax import lax
from jax.experimental.layout import Layout, with_layout_constraint
from jax.experimental import pallas as pl
from jax.experimental.pallas import tpu as pltpu
from jax.sharding import Mesh
from jax.sharding import PartitionSpec as P

ROWS = 9
LANES = 128
F32 = jnp.float32
BF16 = jnp.bfloat16
HIGHEST = lax.Precision.HIGHEST
STATES = 16
LEVELS = 64
M = 40
GROUP = 4
SMALL_VMEM = 24 << 20
LARGE_VMEM = 60 << 20


def iota(shape, dim):
    return lax.broadcasted_iota(jnp.int32, shape, dim)


def exact_dot(a, b):
    return jnp.dot(a, b, precision=HIGHEST, preferred_element_type=F32)


def split(value):
    high = value.astype(BF16)
    return high, (value - high.astype(F32)).astype(BF16)


def dot3(a, b):
    (ah, al), (bh, bl) = a, b
    out = jnp.dot(ah, bl, preferred_element_type=F32) + jnp.dot(al, bh, preferred_element_type=F32)
    return out + jnp.dot(ah, bh, preferred_element_type=F32)


def turn(value, shift):
    shift = shift % LANES
    return pltpu.roll(value, shift, 1) if shift else value


def head_kernel(states_hbm, step_hbm, send_hbm, send_ref, states_ref, step_ref, x_ref, tile_ref, sems):
    step_copy = pltpu.make_async_copy(step_hbm, step_ref, sems.at[2])
    step_copy.start()
    copies = []
    for s in range(2):
        part = pl.ds(s * 1000, 1000)
        copies.append(pltpu.make_async_copy(states_hbm.at[part], states_ref.at[part], sems.at[s]))
        copies[-1].start()
    for e in range(4):
        for row in (16, 40):
            x_ref[e, row : row + 8, :] = jnp.zeros((8, 13 * LANES), F32)
    send_ref[pl.ds(80 * ROWS + 8, 176, stride=ROWS), :] = jnp.zeros((176, LANES), F32)
    row, col = iota((M, M), 0), iota((M, M), 1)
    order = (col == jnp.where(row < 20, 2 * row, 2 * row - 39)).astype(F32)
    row, col = iota((M, 48), 0), iota((M, 48), 1)
    even = (col < 20) & (row == 2 * col)
    odd = (col >= 24) & (col < 44) & (row == 2 * col - 47)
    step_copy.wait()
    step = split(exact_dot(exact_dot(order, step_ref[...]), (even | odd).astype(F32)))

    lane = iota((M, LANES), 1)
    lane20 = iota((20, LANES), 1)
    for s in range(2):
        copies[s].wait()
        for c in range(2):
            e = s * 2 + c

            def tile_in(u):
                return states_ref[pl.ds(s * 1000 + u * 2 + c, 20, stride=50), :]

            for v in range(13):
                x_ref[e, 0:20, v * LANES : (v + 1) * LANES] = tile_in(v)
                low = pltpu.roll(tile_in(12 + v), 64, 1)
                high = pltpu.roll(tile_in(min(13 + v, 24)), 64, 1)
                x_ref[e, 24:44, v * LANES : (v + 1) * LANES] = jnp.where(lane20 < 64, low, high)
            tile_ref[e] = dot3(step, split(x_ref[e]))

    def tile(e, v):
        return tile_ref[e, :, v * LANES : (v + 1) * LANES]

    def chunk(e, m):
        if m == 0:
            return tile(e, 0)
        return jnp.where(lane < 8 * m, turn(tile(e, m - 1), 8 * m), turn(tile(e, m), 8 * m))

    copies = []
    for g in (6, 0, 1, 2, 3, 4, 5):
        extra = jnp.zeros((M, LANES), F32)
        for e in range(4):
            if g == 6:
                last = jnp.where(lane < 120, chunk(e, 12), 0.0)
                for h in range(2):
                    block = last[16 * h : 16 * h + 16]
                    send_ref[pl.ds(240 * ROWS + h * 4 + e, 16, stride=ROWS), :] = block
                continue
            if g == 0:
                seventh = turn(tile(e, 12), -24)
            elif g == 1:
                tail = chunk(e, 12)[32:40]
                tails = [tail, turn(tail, -40), turn(tail, -80), jnp.zeros((16, LANES), F32)]
                seventh = jnp.concatenate(tails, axis=0)
            for h in range(2):
                spare = turn(seventh, 120 - 8 * h) if g < 2 else 0.0
                block = jnp.where(lane < 120, chunk(e, 2 * g + h), spare)
                send_ref[pl.ds(g * M * ROWS + h * 4 + e, M, stride=ROWS), :] = block
            if g < 2:
                inside = (lane >= 32 * e) & (lane < 32 * e + 24)
                extra = jnp.where(inside, turn(seventh, 32 * e - 16), extra)
        if g < 2:
            send_ref[pl.ds(g * M * ROWS + 8, M, stride=ROWS), :] = extra
        part = pl.ds(g * M * ROWS, (M if g < 6 else 16) * ROWS)
        copies.append(pltpu.make_async_copy(send_ref.at[part], send_hbm.at[part], sems.at[3 + g]))
        copies[-1].start()
    for copy in copies:
        copy.wait()


def operands_kernel(
    forward_ref, coupling_ref, mem_forward_ref, back_ref, mem_back_ref,
    cf_ref, cb_ref, mf_ref, mb_ref, ef_ref, eb_ref, w_ref,
):
    def level_of(p):
        return 4 * (p & 15) + 2 * ((p >> 4) & 1) + ((p >> 5) & 1)

    row, lane = iota((LEVELS, 4 * LEVELS), 0), iota((LEVELS, 4 * LEVELS), 1)
    forward = exact_dot(forward_ref[...], (row == level_of(lane & 63)).astype(F32))
    ordered = (iota((LEVELS, LEVELS), 1) == level_of(iota((LEVELS, LEVELS), 0))).astype(F32)
    back = exact_dot(exact_dot(ordered, back_ref[...]), (row == (lane & 63)).astype(F32))
    for ref, value in ((cf_ref, forward), (cb_ref, back)):
        high, low = (part.astype(F32) for part in split(value))
        ref[...] = jnp.where(lane < 128, high, jnp.where(lane < 192, low, 0.0)).astype(BF16)

    def threes(lane):
        third = (lane >= 40).astype(jnp.int32) + (lane >= 80).astype(jnp.int32)
        return jnp.where(lane < 120, third, -1), jnp.where(lane < 120, lane - 40 * third, -1)

    def sevenths(lane):
        real = (lane & 63) < 40
        return jnp.where(real, lane >> 6, -1), jnp.where(real, lane & 63, -1)

    for n, (place, fref, bref) in enumerate(((threes, mf_ref, mb_ref), (sevenths, ef_ref, eb_ref))):
        slot_in, _ = place(iota((LANES, LANES), 0))
        slot_out, _ = place(iota((LANES, LANES), 1))
        same = (slot_in == slot_out) & (slot_in >= 0)
        down = (place(iota((LANES, M), 0))[1] == iota((LANES, M), 1)).astype(F32)
        across = (place(iota((M, LANES), 1))[1] == iota((M, LANES), 0)).astype(F32)
        for ref, matrix in ((fref, mem_forward_ref), (bref, mem_back_ref)):
            turned = lax.dot_general(
                down, matrix[...], (((1,), (1,)), ((), ())), precision=HIGHEST, preferred_element_type=F32
            )
            ref[0], ref[1] = split(jnp.where(same, exact_dot(turned, across), 0.0))
        w_ref[n] = exact_dot(coupling_ref[...], across)


def cavity(matrix, value):
    high, low = split(value)
    out = []
    for row in range(0, value.shape[0], LEVELS):
        h, l = high[row : row + LEVELS], low[row : row + LEVELS]
        stacked = jnp.concatenate([h, l, h, h], axis=0)
        out.append(jnp.dot(matrix, stacked, preferred_element_type=F32))
    return jnp.concatenate(out, axis=0)


def doubled(ref):
    high, low = ref[0], ref[1]
    left = jnp.concatenate([high, high], axis=0)
    right = jnp.concatenate([low, jnp.zeros_like(low)], axis=0)
    return jnp.concatenate([left, right], axis=1)


def membrane(value, matrix):
    out = []
    for lane in range(0, value.shape[1], LANES):
        high, low = split(value[:, lane : lane + LANES])
        both = jnp.dot(jnp.concatenate([high, low], axis=1), matrix, preferred_element_type=F32)
        out.append(both[:, :LANES] + both[:, LANES:])
    return jnp.concatenate(out, axis=1) if len(out) > 1 else out[0]


def flat_place(s, t):
    return (s // 8) * LANES + (-s % 8) * STATES + t


def step_kernel(
    recv_ref, cf_ref, cb_ref, mf_ref, mb_ref, ef_ref, eb_ref, w_ref, main_ref, rest_ref, gram_ref, rows_ref
):
    cf, cb = cf_ref[...], cb_ref[...]
    mf, mb, ef, eb = (doubled(ref) for ref in (mf_ref, mb_ref, ef_ref, eb_ref))
    w_half = jnp.concatenate([w_ref[0]] * GROUP, axis=0)
    w_main = jnp.concatenate([w_half, w_half], axis=1)
    w_rest = jnp.concatenate([w_ref[1]] * GROUP, axis=0)
    size = GROUP * LEVELS
    groups = STATES // GROUP

    lane = iota((32, LANES), 1)
    parts = []
    for part in range(2):
        sevenths = [recv_ref[pl.ds((2 * g + part) * 32 * ROWS + 8, 32, stride=ROWS), :] for g in range(groups)]
        for e in range(4):
            value = turn(sevenths[3], 32 * (3 - e))
            for g in range(2, -1, -1):
                value = jnp.where(lane < 32 * g + 32, turn(sevenths[g], 32 * (g - e)), value)
            parts.append(jnp.where((lane & 31) < 24, value, 0.0))
    rest = cavity(cf, jnp.concatenate(parts, axis=0))

    lane = iota((size, LANES), 1)
    rest_back = jnp.zeros((size, LANES), F32)
    for pair in range(groups // 2):
        mains = []
        extra = jnp.zeros((size, LANES), F32)
        for half in range(2):
            group = 2 * pair + half
            parts = []
            for z in range(group * 2, group * 2 + 2):
                for e in range(4):
                    tiles = [recv_ref[pl.ds(z * 32 * ROWS + h * 4 + e, 32, stride=ROWS), :] for h in range(2)]
                    parts.append(jnp.concatenate(tiles, axis=1))
            value = cavity(cf, jnp.concatenate(parts, axis=0))
            at = 64 * half
            moved = jnp.where(lane < at + 16, turn(value[:, LANES:], at + 16), turn(rest, at + 16 - 32 * group))
            moved = jnp.where(lane < at + 8, turn(value[:, :LANES], at + 8), moved)
            extra = jnp.where((lane >= at) & (lane < at + 40), moved, extra)
            value = membrane(value, mf) * w_main
            mains.append(membrane(value, mb))
        extra = membrane(extra, ef) * w_rest
        extra = membrane(extra, eb)
        for half in range(2):
            group = 2 * pair + half
            at = 64 * half
            tiles = []
            for h in range(2):
                tile = mains[half][:, h * LANES : (h + 1) * LANES]
                tiles.append(jnp.where(lane < 120, tile, turn(extra, 120 - at - 8 * h)))
            value = cavity(cb, jnp.concatenate(tiles, axis=1))
            for h in range(2):
                main_ref[h, group * size : (group + 1) * size, :] = value[:, h * LANES : (h + 1) * LANES]
            inside = (lane >= 32 * group) & (lane < 32 * group + 24)
            rest_back = jnp.where(inside, turn(extra, 32 * group - at - 16), rest_back)
    rest = cavity(cb, rest_back)
    for group in range(groups):
        rest_ref[group * size : (group + 1) * size, :] = jnp.where(lane < 24, turn(rest, -32 * group), 0.0)

    for first in range(0, STATES, 4):
        for second in range(0, first + 4, 4):

            def add(tile, sums, first=first, second=second):
                start = pl.multiple_of(tile * 8, 8)
                for load in (
                    lambda st: main_ref[0, pl.ds(st * LEVELS + start, 8), :],
                    lambda st: main_ref[1, pl.ds(st * LEVELS + start, 8), :],
                    lambda st: rest_ref[pl.ds(st * LEVELS + start, 8), :],
                ):
                    a = [load(first + n) for n in range(4)]
                    b = a if first == second else [load(second + n) for n in range(4)]
                    sums = tuple(sums[p * 4 + q] + a[p] * b[q] for p in range(4) for q in range(4))
                return sums

            sums = lax.fori_loop(0, 8, add, (jnp.zeros((8, LANES), F32),) * 16, unroll=True)
            for p in range(4):
                for q in range(4):
                    total = jnp.sum(sums[p * 4 + q], axis=0, keepdims=True)
                    at = flat_place(first + p, second + q)
                    rows_ref[at : at + 1, :] = total
                    if first != second:
                        at = flat_place(second + q, first + p)
                        rows_ref[at : at + 1, :] = total
    flat = lax.dot_general(
        jnp.ones((32, LANES), F32), rows_ref[...], (((1,), (1,)), ((), ())), precision=HIGHEST,
        preferred_element_type=F32,
    )
    for h in range(2):
        gram_ref[pl.ds(h, 32, stride=2), :] = flat[:, h * LANES : (h + 1) * LANES]


def mix_kernel(scale, gram_ref, main_ref, rest_ref, send_ref, coef_ref):
    gram = gram_ref[0:2, :]
    for z in range(1, 8):
        gram = gram + gram_ref[2 * z : 2 * z + 2, :]
    gram = gram * scale
    square = [
        pltpu.roll(jnp.broadcast_to(gram[h : h + 1], (8, LANES)), 0, 1, stride=16, stride_axis=0)
        for h in range(2)
    ]
    row, col = iota((STATES, LANES), 0), iota((STATES, LANES), 1)
    work = jnp.where(col < STATES, jnp.concatenate(square, axis=0), (col == row + STATES).astype(F32))
    for j in range(STATES - 1):
        pivot = work[j : j + 1, :]
        pivot = pivot * (1.0 / jnp.broadcast_to(pivot[:, j : j + 1], (1, LANES)))
        work = work - jnp.where(row > j, work[:, j : j + 1], 0.0) * pivot
    diagonal = jnp.sum(jnp.where(col == row, work, 0.0), axis=1, keepdims=True)
    inverse = work / jnp.sqrt(diagonal)
    for st in range(STATES):
        column = jnp.broadcast_to(inverse[:, STATES + st : STATES + st + 1], (STATES, LANES))
        coef_ref[st * STATES : (st + 1) * STATES, :] = column

    lane = iota((8, LANES), 1)

    def mixed(loads):
        values = [[load(st) for load in loads] for st in range(STATES)]
        for t in range(STATES):
            sums = [None, None]
            for st in range(t + 1):
                factor = coef_ref[st * STATES + t : st * STATES + t + 1, :]
                for n in range(2):
                    term = factor * values[st][n]
                    sums[n] = term if sums[n] is None else sums[n] + term
            yield t, sums

    def tile(n, carry):
        start = pl.multiple_of(n * 8, 8)
        for c in range(2):
            loads = [
                lambda st, h=h: main_ref[h, pl.ds(st * LEVELS + c * 32 + start, 8), :] for h in range(2)
            ]
            for t, sums in mixed(loads):
                z, s = t // 2, t % 2
                for h in range(2):
                    at = (z * 32 + start) * ROWS + h * 4 + s * 2 + c
                    send_ref[pl.ds(at, 8, stride=ROWS), :] = sums[h]
        loads = [lambda st, c=c: rest_ref[pl.ds(st * LEVELS + c * 32 + start, 8), :] for c in range(2)]
        seventh = None
        for t, sums in mixed(loads):
            z, s = t // 2, t % 2
            for c in range(2):
                e = s * 2 + c
                value = pltpu.roll(sums[c], 32 * e, 1) if e else sums[c]
                seventh = value if e == 0 else seventh + value
            if s == 1:
                send_ref[pl.ds((z * 32 + start) * ROWS + 8, 8, stride=ROWS), :] = seventh
        return carry

    lax.fori_loop(0, 4, tile, 0, unroll=2)


def tail_kernel(recv_ref, out_hbm, out_ref, chunks_ref, tiles_ref, sems):
    copies = []
    lane = iota((M, LANES), 1)
    lane8 = iota((8, LANES), 1)
    lane20 = iota((20, LANES), 1)
    for s in range(2):
        for c in range(2):
            e = s * 2 + c
            chunk_ref, tile_ref = chunks_ref.at[e], tiles_ref.at[e]
            for m in range(12):
                g, h = m // 2, m % 2
                chunk_ref[m] = recv_ref[pl.ds(g * M * ROWS + h * 4 + e, M, stride=ROWS), :]
            for h in range(2):
                chunk_ref[12, 16 * h : 16 * h + 16] = recv_ref[pl.ds(240 * ROWS + h * 4 + e, 16, stride=ROWS), :]
            extras = []
            for g in range(2):
                seventh = recv_ref[pl.ds(g * M * ROWS + 8, M, stride=ROWS), :]
                extra = jnp.where(
                    lane < 8, pltpu.roll(chunk_ref[2 * g], 8, 1), pltpu.roll(chunk_ref[2 * g + 1], 16, 1)
                )
                extras.append(jnp.where(lane < 16, extra, pltpu.roll(seventh, (16 - 32 * e) % LANES, 1)))
            first, second, third = (extras[1][8 * n : 8 * n + 8] for n in range(3))
            chunk_ref[12, 32:40] = jnp.where(
                lane8 < 40,
                first,
                jnp.where(lane8 < 80, pltpu.roll(second, 40, 1), pltpu.roll(third, 80, 1)),
            )
            chunk_ref[13] = extras[0]
            for v in range(13):
                low = pltpu.roll(chunk_ref[v], (LANES - 8 * v) % LANES, 1) if v else chunk_ref[v]
                high = pltpu.roll(chunk_ref[v + 1], 120 - 8 * v, 1)
                tile_ref[v] = jnp.where(lane < 120 - 8 * v, low, high)
            for u in range(25):
                if u < 12:
                    value = tile_ref[u, 0:20]
                else:
                    low = tile_ref[12, 0:20] if u == 12 else pltpu.roll(tile_ref[u - 13, 20:40], 64, 1)
                    high = pltpu.roll(tile_ref[u - 12, 20:40], 64, 1)
                    value = jnp.where(lane20 < 64, low, high)
                out_ref[pl.ds(s * 1000 + u * 2 + c, 20, stride=50), :] = value
        part = pl.ds(s * 1000, 1000)
        copies.append(pltpu.make_async_copy(out_ref.at[part], out_hbm.at[part], sems.at[s]))
        copies[-1].start()
    for copy in copies:
        copy.wait()


def call(kernel, outs, scratch, cost, places="v", limit=SMALL_VMEM, out_place="v"):
    spaces = {"v": pltpu.VMEM, "h": pltpu.HBM}
    return pl.pallas_call(
        kernel,
        out_shape=outs,
        in_specs=[pl.BlockSpec(memory_space=spaces[p]) for p in places],
        out_specs=jax.tree.map(lambda _: pl.BlockSpec(memory_space=spaces[out_place]), outs),
        scratch_shapes=scratch,
        compiler_params=pltpu.CompilerParams(vmem_limit_bytes=limit),
        cost_estimate=pl.CostEstimate(flops=cost, bytes_accessed=1 << 20, transcendentals=0),
    )


def shape(*dims, dtype=F32):
    return jax.ShapeDtypeStruct(dims, dtype)


def exchange(blocks, axes):
    count = 1
    for a in axes:
        count *= lax.axis_size(a)
    rows = blocks.shape[0] // count
    value = blocks.reshape(count, 1, rows * LANES)
    value = lax.all_to_all(value, axes, split_axis=0, concat_axis=0, tiled=True)
    return value.reshape(blocks.shape)


def body(states, membrane_step, cavity_forward, coupling, membrane_forward, cavity_back, membrane_back):
    panel, levels, joint = states.shape
    everyone = ("state", "core", "plane")
    by_tile = Layout(major_to_minor=(0, 2, 1, 3))
    linear = with_layout_constraint(states.reshape(panel, levels, joint // LANES, LANES), by_tile)
    linear = jnp.swapaxes(linear, 1, 2).reshape(-1, LANES)
    blocks = shape(256 * ROWS, LANES)
    send = call(
        head_kernel,
        blocks,
        [
            pltpu.VMEM((256 * ROWS, LANES), F32),
            pltpu.VMEM((2000, LANES), F32),
            pltpu.VMEM((M, M), F32),
            pltpu.VMEM((4, 48, 13 * LANES), F32),
            pltpu.VMEM((4, M, 13 * LANES), F32),
            pltpu.SemaphoreType.DMA((10,)),
        ],
        1 << 20,
        "hh",
        LARGE_VMEM,
        "h",
    )(linear, membrane_step)
    wides = [shape(LEVELS, 4 * LEVELS, dtype=BF16)] * 2
    squares = [shape(2, LANES, LANES, dtype=BF16)] * 4
    operands = call(operands_kernel, (*wides, *squares, shape(2, LEVELS, LANES)), [], 1 << 27, "vvvvv")(
        cavity_forward, coupling, membrane_forward, cavity_back, membrane_back
    )
    recv = exchange(send, everyone)
    main, rest, gram = call(
        step_kernel,
        (shape(2, STATES * LEVELS, LANES), shape(STATES * LEVELS, LANES), shape(64, LANES)),
        [pltpu.VMEM((STATES * STATES, LANES), F32)],
        1 << 30,
        "vvvvvvvv",
    )(recv, *operands)
    gram = lax.all_to_all(gram.reshape(32, 2, LANES), ("plane", "core"), split_axis=0, concat_axis=0, tiled=True)
    gram = jnp.broadcast_to(jnp.sum(gram, axis=0, keepdims=True), (8, 2, LANES))
    gram = lax.all_to_all(gram, "state", split_axis=0, concat_axis=0, tiled=True)
    scale = 1.0 / float(LEVELS * joint)
    send = call(
        lambda *refs: mix_kernel(scale, *refs),
        blocks,
        [pltpu.VMEM((STATES * STATES, LANES), F32)],
        1 << 27,
        "vvv",
    )(gram.reshape(16, LANES), main, rest)
    recv = exchange(send, everyone)
    out = call(
        tail_kernel,
        shape(2000, LANES),
        [
            pltpu.VMEM((2000, LANES), F32),
            pltpu.VMEM((4, 14, M, LANES), F32),
            pltpu.VMEM((4, 13, M, LANES), F32),
            pltpu.SemaphoreType.DMA((2,)),
        ],
        1 << 20,
        out_place="h",
    )(recv)
    out = out.reshape(panel, joint // LANES, levels, LANES)
    return with_layout_constraint(jnp.swapaxes(out, 1, 2), by_tile).reshape(panel, levels, joint)


def solution(mesh):
    states = mesh.shape["state"]
    cores = Mesh(mesh.devices.reshape(states, -1, 2), ("state", "plane", "core"))
    out_specs = P("state", ("plane", "core"), None)
    in_specs = (out_specs, P(), P(), P(), P(), P(), P())
    return jax.shard_map(body, mesh=cores, in_specs=in_specs, out_specs=out_specs, check_vma=False)
```

```python
import jax
import jax.numpy as jnp
from jax import lax
from jax.experimental.layout import Layout, with_layout_constraint
from jax.experimental import pallas as pl
from jax.experimental.pallas import tpu as pltpu
from jax.sharding import Mesh
from jax.sharding import PartitionSpec as P

ROWS = 9
LANES = 128
F32 = jnp.float32
BF16 = jnp.bfloat16
HIGHEST = lax.Precision.HIGHEST
STATES = 16
LEVELS = 64
M = 40
GROUP = 4
SMALL_VMEM = 24 << 20
LARGE_VMEM = 60 << 20


def iota(shape, dim):
    return lax.broadcasted_iota(jnp.int32, shape, dim)


def exact_dot(a, b):
    return jnp.dot(a, b, precision=HIGHEST, preferred_element_type=F32)


def split(value):
    high = value.astype(BF16)
    return high, (value - high.astype(F32)).astype(BF16)


def dot3(a, b):
    (ah, al), (bh, bl) = a, b
    out = jnp.dot(ah, bl, preferred_element_type=F32) + jnp.dot(al, bh, preferred_element_type=F32)
    return out + jnp.dot(ah, bh, preferred_element_type=F32)


def turn(value, shift):
    shift = shift % LANES
    return pltpu.roll(value, shift, 1) if shift else value


def head_kernel(states_hbm, step_hbm, send_hbm, send_ref, states_ref, step_ref, x_ref, tile_ref, sems):
    step_copy = pltpu.make_async_copy(step_hbm, step_ref, sems.at[2])
    step_copy.start()
    copies = []
    for s in range(2):
        part = pl.ds(s * 1000, 1000)
        copies.append(pltpu.make_async_copy(states_hbm.at[part], states_ref.at[part], sems.at[s]))
        copies[-1].start()
    for e in range(4):
        for row in (16, 40):
            x_ref[e, row : row + 8, :] = jnp.zeros((8, 13 * LANES), F32)
    send_ref[pl.ds(80 * ROWS + 8, 176, stride=ROWS), :] = jnp.zeros((176, LANES), F32)
    row, col = iota((M, M), 0), iota((M, M), 1)
    order = (col == jnp.where(row < 20, 2 * row, 2 * row - 39)).astype(F32)
    row, col = iota((M, 48), 0), iota((M, 48), 1)
    even = (col < 20) & (row == 2 * col)
    odd = (col >= 24) & (col < 44) & (row == 2 * col - 47)
    step_copy.wait()
    step = split(exact_dot(exact_dot(order, step_ref[...]), (even | odd).astype(F32)))

    lane = iota((M, LANES), 1)
    lane20 = iota((20, LANES), 1)
    for s in range(2):
        copies[s].wait()
        for c in range(2):
            e = s * 2 + c

            def tile_in(u):
                return states_ref[pl.ds(s * 1000 + u * 2 + c, 20, stride=50), :]

            for v in range(13):
                x_ref[e, 0:20, v * LANES : (v + 1) * LANES] = tile_in(v)
                odd = jnp.where(lane20 < 64, tile_in(min(13 + v, 24)), tile_in(12 + v))
                x_ref[e, 24:44, v * LANES : (v + 1) * LANES] = turn(odd, 64)
            tile_ref[e] = dot3(step, split(x_ref[e]))

    def tile(e, v):
        return tile_ref[e, :, v * LANES : (v + 1) * LANES]

    def chunk(e, m):
        if m == 0:
            return tile(e, 0)
        return turn(jnp.where(lane < LANES - 8 * m, tile(e, m), tile(e, m - 1)), 8 * m)

    copies = []
    for g in (6, 0, 1, 2, 3, 4, 5):
        extra = jnp.zeros((M, LANES), F32)
        for e in range(4):
            if g == 6:
                last = jnp.where(lane < 120, chunk(e, 12), 0.0)
                for h in range(2):
                    block = last[16 * h : 16 * h + 16]
                    send_ref[pl.ds(240 * ROWS + h * 4 + e, 16, stride=ROWS), :] = block
                continue
            if g == 0:
                seventh = turn(tile(e, 12), -24)
            elif g == 1:
                tail = chunk(e, 12)[32:40]
                tails = [tail, turn(tail, -40), turn(tail, -80), jnp.zeros((16, LANES), F32)]
                seventh = jnp.concatenate(tails, axis=0)
            for h in range(2):
                spare = turn(seventh, 120 - 8 * h) if g < 2 else 0.0
                block = jnp.where(lane < 120, chunk(e, 2 * g + h), spare)
                send_ref[pl.ds(g * M * ROWS + h * 4 + e, M, stride=ROWS), :] = block
            if g < 2:
                inside = (lane >= 32 * e) & (lane < 32 * e + 24)
                extra = jnp.where(inside, turn(seventh, 32 * e - 16), extra)
        if g < 2:
            send_ref[pl.ds(g * M * ROWS + 8, M, stride=ROWS), :] = extra
        part = pl.ds(g * M * ROWS, (M if g < 6 else 16) * ROWS)
        copies.append(pltpu.make_async_copy(send_ref.at[part], send_hbm.at[part], sems.at[3 + g]))
        copies[-1].start()
    for copy in copies:
        copy.wait()


def operands_kernel(
    forward_ref, coupling_ref, mem_forward_ref, back_ref, mem_back_ref,
    cf_ref, cb_ref, mf_ref, mb_ref, ef_ref, eb_ref, w_ref,
):
    def level_of(p):
        return 4 * (p & 15) + 2 * ((p >> 4) & 1) + ((p >> 5) & 1)

    row, lane = iota((LEVELS, 4 * LEVELS), 0), iota((LEVELS, 4 * LEVELS), 1)
    forward = exact_dot(forward_ref[...], (row == level_of(lane & 63)).astype(F32))
    ordered = (iota((LEVELS, LEVELS), 1) == level_of(iota((LEVELS, LEVELS), 0))).astype(F32)
    back = exact_dot(exact_dot(ordered, back_ref[...]), (row == (lane & 63)).astype(F32))
    for ref, value in ((cf_ref, forward), (cb_ref, back)):
        high, low = (part.astype(F32) for part in split(value))
        ref[...] = jnp.where(lane < 128, high, jnp.where(lane < 192, low, 0.0)).astype(BF16)

    def threes(lane):
        third = (lane >= 40).astype(jnp.int32) + (lane >= 80).astype(jnp.int32)
        return jnp.where(lane < 120, third, -1), jnp.where(lane < 120, lane - 40 * third, -1)

    def sevenths(lane):
        real = (lane & 63) < 40
        return jnp.where(real, lane >> 6, -1), jnp.where(real, lane & 63, -1)

    for n, (place, fref, bref) in enumerate(((threes, mf_ref, mb_ref), (sevenths, ef_ref, eb_ref))):
        slot_in, _ = place(iota((LANES, LANES), 0))
        slot_out, _ = place(iota((LANES, LANES), 1))
        same = (slot_in == slot_out) & (slot_in >= 0)
        down = (place(iota((LANES, M), 0))[1] == iota((LANES, M), 1)).astype(F32)
        across = (place(iota((M, LANES), 1))[1] == iota((M, LANES), 0)).astype(F32)
        for ref, matrix in ((fref, mem_forward_ref), (bref, mem_back_ref)):
            turned = lax.dot_general(
                down, matrix[...], (((1,), (1,)), ((), ())), precision=HIGHEST, preferred_element_type=F32
            )
            ref[0], ref[1] = split(jnp.where(same, exact_dot(turned, across), 0.0))
        w_ref[n] = exact_dot(coupling_ref[...], across)


def cavity(matrix, value):
    high, low = split(value)
    out = []
    for row in range(0, value.shape[0], LEVELS):
        h, l = high[row : row + LEVELS], low[row : row + LEVELS]
        stacked = jnp.concatenate([h, l, h, h], axis=0)
        out.append(jnp.dot(matrix, stacked, preferred_element_type=F32))
    return jnp.concatenate(out, axis=0)


def doubled(ref):
    high, low = ref[0], ref[1]
    left = jnp.concatenate([high, high], axis=0)
    right = jnp.concatenate([low, jnp.zeros_like(low)], axis=0)
    return jnp.concatenate([left, right], axis=1)


def membrane(value, matrix):
    out = []
    for lane in range(0, value.shape[1], LANES):
        high, low = split(value[:, lane : lane + LANES])
        both = jnp.dot(jnp.concatenate([high, low], axis=1), matrix, preferred_element_type=F32)
        out.append(both[:, :LANES] + both[:, LANES:])
    return jnp.concatenate(out, axis=1) if len(out) > 1 else out[0]


def flat_place(s, t):
    return (s // 8) * LANES + (-s % 8) * STATES + t


def step_kernel(
    recv_ref, cf_ref, cb_ref, mf_ref, mb_ref, ef_ref, eb_ref, w_ref, main_ref, rest_ref, gram_ref, rows_ref
):
    cf, cb = cf_ref[...], cb_ref[...]
    mf, mb, ef, eb = (doubled(ref) for ref in (mf_ref, mb_ref, ef_ref, eb_ref))
    w_half = jnp.concatenate([w_ref[0]] * GROUP, axis=0)
    w_main = jnp.concatenate([w_half, w_half], axis=1)
    w_rest = jnp.concatenate([w_ref[1]] * GROUP, axis=0)
    size = GROUP * LEVELS
    groups = STATES // GROUP

    lane = short = iota((32, LANES), 1)
    parts = []
    for part in range(2):
        sevenths = [recv_ref[pl.ds((2 * g + part) * 32 * ROWS + 8, 32, stride=ROWS), :] for g in range(groups)]
        for e in range(4):
            value = turn(sevenths[3], 32 * (3 - e))
            for g in range(2, -1, -1):
                value = jnp.where(lane < 32 * g + 32, turn(sevenths[g], 32 * (g - e)), value)
            parts.append(jnp.where((lane & 31) < 24, value, 0.0))
    rest = cavity(cf, jnp.concatenate(parts, axis=0))

    lane = iota((size, LANES), 1)
    rest_back = jnp.zeros((size, LANES), F32)
    for pair in range(groups // 2):
        mains = []
        extra = jnp.zeros((size, LANES), F32)
        for half in range(2):
            group = 2 * pair + half
            parts = []
            for z in range(group * 2, group * 2 + 2):
                for e in range(4):
                    tiles = [recv_ref[pl.ds(z * 32 * ROWS + h * 4 + e, 32, stride=ROWS), :] for h in range(2)]
                    parts.append(jnp.concatenate(tiles, axis=1))
            value = cavity(cf, jnp.concatenate(parts, axis=0))
            at = 64 * half
            moved = jnp.where(lane < at + 16, turn(value[:, LANES:], at + 16), turn(rest, at + 16 - 32 * group))
            moved = jnp.where(lane < at + 8, turn(value[:, :LANES], at + 8), moved)
            extra = jnp.where((lane >= at) & (lane < at + 40), moved, extra)
            value = membrane(value, mf) * w_main
            mains.append(membrane(value, mb))
        extra = membrane(extra, ef) * w_rest
        extra = membrane(extra, eb)
        for half in range(2):
            group = 2 * pair + half
            at = 64 * half
            tiles = []
            for h in range(2):
                tile = mains[half][:, h * LANES : (h + 1) * LANES]
                tiles.append(jnp.where(lane < 120, tile, turn(extra, 120 - at - 8 * h)))
            value = cavity(cb, jnp.concatenate(tiles, axis=1))
            for h in range(2):
                main_ref[h, group * size : (group + 1) * size, :] = value[:, h * LANES : (h + 1) * LANES]
            inside = (lane >= 32 * group) & (lane < 32 * group + 24)
            rest_back = jnp.where(inside, turn(extra, 32 * group - at - 16), rest_back)
    rest = cavity(cb, rest_back)
    for group in range(groups):
        for st in range(GROUP):
            level = [rest[st * LEVELS + 32 * c : st * LEVELS + 32 * c + 32] for c in range(2)]
            value = jnp.where(short < 24, turn(level[0], -32 * group), 0.0)
            value = jnp.where((short >= 32) & (short < 56), turn(level[1], 32 - 32 * group), value)
            at = (group * GROUP + st) * 32
            rest_ref[at : at + 32, :] = value

    for first in range(0, STATES, 4):
        for second in range(0, first + 4, 4):

            def add(tile, sums, load):
                a = [load(first + n, tile) for n in range(4)]
                b = a if first == second else [load(second + n, tile) for n in range(4)]
                return tuple(sums[p * 4 + q] + a[p] * b[q] for p in range(4) for q in range(4))

            sums = (jnp.zeros((8, LANES), F32),) * 16
            for tile in range(8):
                for h in range(2):
                    sums = add(tile, sums, lambda st, n: main_ref[h, st * LEVELS + n * 8 : st * LEVELS + n * 8 + 8, :])
            for tile in range(4):
                sums = add(tile, sums, lambda st, n: rest_ref[st * 32 + n * 8 : st * 32 + n * 8 + 8, :])
            for p in range(4):
                for q in range(4):
                    total = jnp.sum(sums[p * 4 + q], axis=0, keepdims=True)
                    at = flat_place(first + p, second + q)
                    rows_ref[at : at + 1, :] = total
                    if first != second:
                        at = flat_place(second + q, first + p)
                        rows_ref[at : at + 1, :] = total
    flat = lax.dot_general(
        jnp.ones((32, LANES), F32), rows_ref[...], (((1,), (1,)), ((), ())), precision=HIGHEST,
        preferred_element_type=F32,
    )
    for h in range(2):
        gram_ref[pl.ds(h, 32, stride=2), :] = flat[:, h * LANES : (h + 1) * LANES]


def mix_kernel(scale, gram_ref, main_ref, rest_ref, send_ref, coef_ref):
    gram = gram_ref[0:2, :]
    for z in range(1, 8):
        gram = gram + gram_ref[2 * z : 2 * z + 2, :]
    gram = gram * scale
    square = [
        pltpu.roll(jnp.broadcast_to(gram[h : h + 1], (8, LANES)), 0, 1, stride=16, stride_axis=0)
        for h in range(2)
    ]
    row, col = iota((STATES, LANES), 0), iota((STATES, LANES), 1)
    work = jnp.where(col < STATES, jnp.concatenate(square, axis=0), (col == row + STATES).astype(F32))
    def lanes(value, j):
        return jnp.broadcast_to(value[:, j : j + 1], (value.shape[0], LANES))

    for j in range(0, STATES, 2):
        first, second = work[j : j + 1, :], work[j + 1 : j + 2, :]
        left, right = lanes(work, j), lanes(work, j + 1)
        side = lanes(first, j + 1)
        over = 1.0 / lanes(first, j)
        factor = side * over
        below = 1.0 / (lanes(second, j + 1) - side * factor)
        second = (second - factor * first) * below
        right = right - left * factor
        work = work - jnp.where(row > j, left, 0.0) * (first * over) - jnp.where(row > j + 1, right, 0.0) * second
    diagonal = jnp.sum(jnp.where(col == row, work, 0.0), axis=1, keepdims=True)
    inverse = work / jnp.sqrt(diagonal)
    for st in range(STATES):
        column = jnp.broadcast_to(inverse[:, STATES + st : STATES + st + 1], (STATES, LANES))
        coef_ref[st * STATES : (st + 1) * STATES, :] = column

    lane = iota((8, LANES), 1)

    def mixed(loads):
        values = [[load(st) for load in loads] for st in range(STATES)]
        for t in range(STATES):
            sums = [None] * len(loads)
            for st in range(t + 1):
                factor = coef_ref[st * STATES + t : st * STATES + t + 1, :]
                for n in range(len(loads)):
                    term = factor * values[st][n]
                    sums[n] = term if sums[n] is None else sums[n] + term
            yield t, sums

    def tile(n, carry):
        start = pl.multiple_of(n * 8, 8)
        for c in range(2):
            loads = [
                lambda st, h=h: main_ref[h, pl.ds(st * LEVELS + c * 32 + start, 8), :] for h in range(2)
            ]
            for t, sums in mixed(loads):
                z, s = t // 2, t % 2
                for h in range(2):
                    at = (z * 32 + start) * ROWS + h * 4 + s * 2 + c
                    send_ref[pl.ds(at, 8, stride=ROWS), :] = sums[h]
        loads = [lambda st: rest_ref[pl.ds(st * 32 + start, 8), :]]
        seventh = None
        for t, sums in mixed(loads):
            z, s = t // 2, t % 2
            if s == 0:
                seventh = sums[0]
            else:
                seventh = seventh + turn(sums[0], 64)
                send_ref[pl.ds((z * 32 + start) * ROWS + 8, 8, stride=ROWS), :] = seventh
        return carry

    lax.fori_loop(0, 4, tile, 0, unroll=2)


def tail_kernel(recv_ref, out_hbm, out_ref, chunks_ref, tiles_ref, sems):
    copies = []
    lane = iota((M, LANES), 1)
    lane8 = iota((8, LANES), 1)
    lane20 = iota((20, LANES), 1)
    for s in range(2):
        for c in range(2):
            e = s * 2 + c
            chunk_ref, tile_ref = chunks_ref.at[e], tiles_ref.at[e]
            for m in range(12):
                g, h = m // 2, m % 2
                chunk_ref[m] = recv_ref[pl.ds(g * M * ROWS + h * 4 + e, M, stride=ROWS), :]
            for h in range(2):
                chunk_ref[12, 16 * h : 16 * h + 16] = recv_ref[pl.ds(240 * ROWS + h * 4 + e, 16, stride=ROWS), :]
            extras = []
            for g in range(2):
                seventh = recv_ref[pl.ds(g * M * ROWS + 8, M, stride=ROWS), :]
                extra = jnp.where(
                    lane < 8, pltpu.roll(chunk_ref[2 * g], 8, 1), pltpu.roll(chunk_ref[2 * g + 1], 16, 1)
                )
                extras.append(jnp.where(lane < 16, extra, pltpu.roll(seventh, (16 - 32 * e) % LANES, 1)))
            first, second, third = (extras[1][8 * n : 8 * n + 8] for n in range(3))
            chunk_ref[12, 32:40] = jnp.where(
                lane8 < 40,
                first,
                jnp.where(lane8 < 80, pltpu.roll(second, 40, 1), pltpu.roll(third, 80, 1)),
            )
            chunk_ref[13] = extras[0]
            for v in range(13):
                low = pltpu.roll(chunk_ref[v], (LANES - 8 * v) % LANES, 1) if v else chunk_ref[v]
                high = pltpu.roll(chunk_ref[v + 1], 120 - 8 * v, 1)
                tile_ref[v] = jnp.where(lane < 120 - 8 * v, low, high)
            for u in range(25):
                if u < 12:
                    value = tile_ref[u, 0:20]
                elif u == 12:
                    value = jnp.where(lane20 < 64, tile_ref[12, 0:20], turn(tile_ref[0, 20:40], 64))
                else:
                    value = turn(jnp.where(lane20 < 64, tile_ref[u - 12, 20:40], tile_ref[u - 13, 20:40]), 64)
                out_ref[pl.ds(s * 1000 + u * 2 + c, 20, stride=50), :] = value
        part = pl.ds(s * 1000, 1000)
        copies.append(pltpu.make_async_copy(out_ref.at[part], out_hbm.at[part], sems.at[s]))
        copies[-1].start()
    for copy in copies:
        copy.wait()


def call(kernel, outs, scratch, cost, places="v", limit=SMALL_VMEM, out_place="v"):
    spaces = {"v": pltpu.VMEM, "h": pltpu.HBM}
    return pl.pallas_call(
        kernel,
        out_shape=outs,
        in_specs=[pl.BlockSpec(memory_space=spaces[p]) for p in places],
        out_specs=jax.tree.map(lambda _: pl.BlockSpec(memory_space=spaces[out_place]), outs),
        scratch_shapes=scratch,
        compiler_params=pltpu.CompilerParams(vmem_limit_bytes=limit),
        cost_estimate=pl.CostEstimate(flops=cost, bytes_accessed=1 << 20, transcendentals=0),
    )


def shape(*dims, dtype=F32):
    return jax.ShapeDtypeStruct(dims, dtype)


def exchange(blocks, axes):
    count = 1
    for a in axes:
        count *= lax.axis_size(a)
    rows = blocks.shape[0] // count
    value = blocks.reshape(count, 1, rows * LANES)
    value = lax.all_to_all(value, axes, split_axis=0, concat_axis=0, tiled=True)
    return value.reshape(blocks.shape)


def body(states, membrane_step, cavity_forward, coupling, membrane_forward, cavity_back, membrane_back):
    panel, levels, joint = states.shape
    everyone = ("state", "core", "plane")
    by_tile = Layout(major_to_minor=(0, 2, 1, 3))
    linear = with_layout_constraint(states.reshape(panel, levels, joint // LANES, LANES), by_tile)
    linear = jnp.swapaxes(linear, 1, 2).reshape(-1, LANES)
    blocks = shape(256 * ROWS, LANES)
    send = call(
        head_kernel,
        blocks,
        [
            pltpu.VMEM((256 * ROWS, LANES), F32),
            pltpu.VMEM((2208, LANES), F32),
            pltpu.VMEM((M, M), F32),
            pltpu.VMEM((4, 48, 13 * LANES), F32),
            pltpu.VMEM((4, M, 13 * LANES), F32),
            pltpu.SemaphoreType.DMA((10,)),
        ],
        1 << 20,
        "hh",
        LARGE_VMEM,
        "h",
    )(linear, membrane_step)
    wides = [shape(LEVELS, 4 * LEVELS, dtype=BF16)] * 2
    squares = [shape(2, LANES, LANES, dtype=BF16)] * 4
    operands = call(operands_kernel, (*wides, *squares, shape(2, LEVELS, LANES)), [], 1 << 27, "vvvvv")(
        cavity_forward, coupling, membrane_forward, cavity_back, membrane_back
    )
    recv = exchange(send, everyone)
    main, rest, gram = call(
        step_kernel,
        (shape(2, STATES * LEVELS, LANES), shape(STATES * 32, LANES), shape(64, LANES)),
        [pltpu.VMEM((STATES * STATES, LANES), F32)],
        1 << 30,
        "vvvvvvvv",
    )(recv, *operands)
    gram = lax.all_to_all(gram.reshape(32, 2, LANES), ("plane", "core"), split_axis=0, concat_axis=0, tiled=True)
    gram = jnp.broadcast_to(jnp.sum(gram, axis=0, keepdims=True), (8, 2, LANES))
    gram = lax.all_to_all(gram, "state", split_axis=0, concat_axis=0, tiled=True)
    scale = 1.0 / float(LEVELS * joint)
    send = call(
        lambda *refs: mix_kernel(scale, *refs),
        blocks,
        [pltpu.VMEM((STATES * STATES, LANES), F32)],
        1 << 27,
        "vvv",
    )(gram.reshape(16, LANES), main, rest)
    recv = exchange(send, everyone)
    out = call(
        tail_kernel,
        shape(2000, LANES),
        [
            pltpu.VMEM((2208, LANES), F32),
            pltpu.VMEM((4, 14, M, LANES), F32),
            pltpu.VMEM((4, 13, M, LANES), F32),
            pltpu.SemaphoreType.DMA((2,)),
        ],
        1 << 20,
        out_place="h",
    )(recv)
    out = out.reshape(panel, joint // LANES, levels, LANES)
    return with_layout_constraint(jnp.swapaxes(out, 1, 2), by_tile).reshape(panel, levels, joint)


def solution(mesh):
    states = mesh.shape["state"]
    cores = Mesh(mesh.devices.reshape(states, -1, 2), ("state", "plane", "core"))
    out_specs = P("state", ("plane", "core"), None)
    in_specs = (out_specs, P(), P(), P(), P(), P(), P())
    return jax.shard_map(body, mesh=cores, in_specs=in_specs, out_specs=out_specs, check_vma=False)
```

```python
import jax
import jax.numpy as jnp
from jax import lax
from jax.experimental.layout import Layout, with_layout_constraint
from jax.experimental import pallas as pl
from jax.experimental.pallas import tpu as pltpu
from jax.sharding import Mesh
from jax.sharding import PartitionSpec as P

ROWS = 9
LANES = 128
F32 = jnp.float32
BF16 = jnp.bfloat16
HIGHEST = lax.Precision.HIGHEST
STATES = 16
LEVELS = 64
M = 40
GROUP = 4
SMALL_VMEM = 24 << 20
LARGE_VMEM = 60 << 20


def iota(shape, dim):
    return lax.broadcasted_iota(jnp.int32, shape, dim)


def exact_dot(a, b):
    return jnp.dot(a, b, precision=HIGHEST, preferred_element_type=F32)


def split(value):
    high = value.astype(BF16)
    return high, (value - high.astype(F32)).astype(BF16)


def dot3(a, b):
    (ah, al), (bh, bl) = a, b
    out = jnp.dot(ah, bl, preferred_element_type=F32) + jnp.dot(al, bh, preferred_element_type=F32)
    return out + jnp.dot(ah, bh, preferred_element_type=F32)


def turn(value, shift):
    shift = shift % LANES
    return pltpu.roll(value, shift, 1) if shift else value


def head_kernel(states_hbm, step_hbm, send_hbm, send_ref, states_ref, step_ref, x_ref, tile_ref, sems):
    step_copy = pltpu.make_async_copy(step_hbm, step_ref, sems.at[2])
    step_copy.start()
    copies = []
    for s in range(2):
        part = pl.ds(s * 1000, 1000)
        copies.append(pltpu.make_async_copy(states_hbm.at[part], states_ref.at[part], sems.at[s]))
        copies[-1].start()
    for e in range(4):
        for row in (16, 40):
            x_ref[e, row : row + 8, :] = jnp.zeros((8, 14 * LANES), F32)
    send_ref[pl.ds(80 * ROWS + 8, 176, stride=ROWS), :] = jnp.zeros((176, LANES), F32)
    row, col = iota((M, M), 0), iota((M, M), 1)
    order = (col == jnp.where(row < 20, 2 * row, 2 * row - 39)).astype(F32)
    row, col = iota((M, 48), 0), iota((M, 48), 1)
    even = (col < 20) & (row == 2 * col)
    odd = (col >= 24) & (col < 44) & (row == 2 * col - 47)
    step_copy.wait()
    step = split(exact_dot(exact_dot(order, step_ref[...]), (even | odd).astype(F32)))

    lane = iota((M, LANES), 1)
    lane20 = iota((20, LANES), 1)
    for s in range(2):
        copies[s].wait()
        for c in range(2):
            e = s * 2 + c

            def tile_in(u):
                return states_ref[pl.ds(s * 1000 + u * 2 + c, 20, stride=50), :]

            for m in range(14):
                at = slice(m * LANES, (m + 1) * LANES)
                value = tile_in(0)
                if m:
                    value = turn(jnp.where(lane20 < LANES - 8 * m, tile_in(m), tile_in(m - 1)), 8 * m)
                x_ref[e, 0:20, at] = value
                first, offset = divmod(1600 + 120 * m, LANES)
                value = jnp.where(lane20 >= offset, tile_in(first), tile_in(min(first + 1, 24)))
                x_ref[e, 24:44, at] = turn(value, -offset)
            tile_ref[e] = dot3(step, split(x_ref[e]))

    def chunk(e, m):
        return tile_ref[e, :, m * LANES : (m + 1) * LANES]

    copies = []
    for g in (6, 0, 1, 2, 3, 4, 5):
        extra = jnp.zeros((M, LANES), F32)
        for e in range(4):
            if g == 6:
                last = jnp.where(lane < 120, chunk(e, 12), 0.0)
                for h in range(2):
                    block = last[16 * h : 16 * h + 16]
                    send_ref[pl.ds(240 * ROWS + h * 4 + e, 16, stride=ROWS), :] = block
                continue
            if g == 0:
                seventh = chunk(e, 13)
            elif g == 1:
                tail = chunk(e, 12)[32:40]
                tails = [tail, turn(tail, -40), turn(tail, -80), jnp.zeros((16, LANES), F32)]
                seventh = jnp.concatenate(tails, axis=0)
            for h in range(2):
                spare = turn(seventh, 120 - 8 * h) if g < 2 else 0.0
                block = jnp.where(lane < 120, chunk(e, 2 * g + h), spare)
                send_ref[pl.ds(g * M * ROWS + h * 4 + e, M, stride=ROWS), :] = block
            if g < 2:
                inside = (lane >= 32 * e) & (lane < 32 * e + 24)
                extra = jnp.where(inside, turn(seventh, 32 * e - 16), extra)
        if g < 2:
            send_ref[pl.ds(g * M * ROWS + 8, M, stride=ROWS), :] = extra
        part = pl.ds(g * M * ROWS, (M if g < 6 else 16) * ROWS)
        copies.append(pltpu.make_async_copy(send_ref.at[part], send_hbm.at[part], sems.at[3 + g]))
        copies[-1].start()
    for copy in copies:
        copy.wait()


def operands_kernel(
    forward_ref, coupling_ref, mem_forward_ref, back_ref, mem_back_ref,
    cf_ref, cb_ref, mf_ref, mb_ref, ef_ref, eb_ref, w_ref,
):
    def level_of(p):
        return 4 * (p & 15) + 2 * ((p >> 4) & 1) + ((p >> 5) & 1)

    row, lane = iota((LEVELS, 4 * LEVELS), 0), iota((LEVELS, 4 * LEVELS), 1)
    forward = exact_dot(forward_ref[...], (row == level_of(lane & 63)).astype(F32))
    ordered = (iota((LEVELS, LEVELS), 1) == level_of(iota((LEVELS, LEVELS), 0))).astype(F32)
    back = exact_dot(exact_dot(ordered, back_ref[...]), (row == (lane & 63)).astype(F32))
    for ref, value in ((cf_ref, forward), (cb_ref, back)):
        high, low = (part.astype(F32) for part in split(value))
        ref[...] = jnp.where(lane < 128, high, jnp.where(lane < 192, low, 0.0)).astype(BF16)

    def threes(lane):
        third = (lane >= 40).astype(jnp.int32) + (lane >= 80).astype(jnp.int32)
        return jnp.where(lane < 120, third, -1), jnp.where(lane < 120, lane - 40 * third, -1)

    def sevenths(lane):
        real = (lane & 63) < 40
        return jnp.where(real, lane >> 6, -1), jnp.where(real, lane & 63, -1)

    for n, (place, fref, bref) in enumerate(((threes, mf_ref, mb_ref), (sevenths, ef_ref, eb_ref))):
        slot_in, _ = place(iota((LANES, LANES), 0))
        slot_out, _ = place(iota((LANES, LANES), 1))
        same = (slot_in == slot_out) & (slot_in >= 0)
        down = (place(iota((LANES, M), 0))[1] == iota((LANES, M), 1)).astype(F32)
        across = (place(iota((M, LANES), 1))[1] == iota((M, LANES), 0)).astype(F32)
        for ref, matrix in ((fref, mem_forward_ref), (bref, mem_back_ref)):
            turned = lax.dot_general(
                down, matrix[...], (((1,), (1,)), ((), ())), precision=HIGHEST, preferred_element_type=F32
            )
            ref[0], ref[1] = split(jnp.where(same, exact_dot(turned, across), 0.0))
        w_ref[n] = exact_dot(coupling_ref[...], across)


def cavity(matrix, value):
    high, low = split(value)
    out = []
    for row in range(0, value.shape[0], LEVELS):
        h, l = high[row : row + LEVELS], low[row : row + LEVELS]
        stacked = jnp.concatenate([h, l, h, h], axis=0)
        out.append(jnp.dot(matrix, stacked, preferred_element_type=F32))
    return jnp.concatenate(out, axis=0)


def doubled(ref):
    high, low = ref[0], ref[1]
    left = jnp.concatenate([high, high], axis=0)
    right = jnp.concatenate([low, jnp.zeros_like(low)], axis=0)
    return jnp.concatenate([left, right], axis=1)


def membrane(value, matrix):
    out = []
    for lane in range(0, value.shape[1], LANES):
        high, low = split(value[:, lane : lane + LANES])
        both = jnp.dot(jnp.concatenate([high, low], axis=1), matrix, preferred_element_type=F32)
        out.append(both[:, :LANES] + both[:, LANES:])
    return jnp.concatenate(out, axis=1) if len(out) > 1 else out[0]


def flat_place(s, t):
    return (s // 8) * LANES + (-s % 8) * STATES + t


def step_kernel(
    recv_ref, cf_ref, cb_ref, mf_ref, mb_ref, ef_ref, eb_ref, w_ref, main_ref, rest_ref, gram_ref, rows_ref
):
    cf, cb = cf_ref[...], cb_ref[...]
    mf, mb, ef, eb = (doubled(ref) for ref in (mf_ref, mb_ref, ef_ref, eb_ref))
    w_half = jnp.concatenate([w_ref[0]] * GROUP, axis=0)
    w_main = jnp.concatenate([w_half, w_half], axis=1)
    w_rest = jnp.concatenate([w_ref[1]] * GROUP, axis=0)
    size = GROUP * LEVELS
    groups = STATES // GROUP

    lane = short = iota((32, LANES), 1)
    parts = []
    for part in range(2):
        sevenths = [recv_ref[pl.ds((2 * g + part) * 32 * ROWS + 8, 32, stride=ROWS), :] for g in range(groups)]
        for e in range(4):
            value = turn(sevenths[3], 32 * (3 - e))
            for g in range(2, -1, -1):
                value = jnp.where(lane < 32 * g + 32, turn(sevenths[g], 32 * (g - e)), value)
            parts.append(jnp.where((lane & 31) < 24, value, 0.0))
    rest = cavity(cf, jnp.concatenate(parts, axis=0))

    lane = iota((size, LANES), 1)
    rest_back = jnp.zeros((size, LANES), F32)
    for pair in range(groups // 2):
        mains = []
        extra = jnp.zeros((size, LANES), F32)
        for half in range(2):
            group = 2 * pair + half
            parts = []
            for z in range(group * 2, group * 2 + 2):
                for e in range(4):
                    tiles = [recv_ref[pl.ds(z * 32 * ROWS + h * 4 + e, 32, stride=ROWS), :] for h in range(2)]
                    parts.append(jnp.concatenate(tiles, axis=1))
            value = cavity(cf, jnp.concatenate(parts, axis=0))
            at = 64 * half
            moved = jnp.where(lane < at + 16, turn(value[:, LANES:], at + 16), turn(rest, at + 16 - 32 * group))
            moved = jnp.where(lane < at + 8, turn(value[:, :LANES], at + 8), moved)
            extra = jnp.where((lane >= at) & (lane < at + 40), moved, extra)
            value = membrane(value, mf) * w_main
            mains.append(membrane(value, mb))
        extra = membrane(extra, ef) * w_rest
        extra = membrane(extra, eb)
        for half in range(2):
            group = 2 * pair + half
            at = 64 * half
            tiles = []
            for h in range(2):
                tile = mains[half][:, h * LANES : (h + 1) * LANES]
                tiles.append(jnp.where(lane < 120, tile, turn(extra, 120 - at - 8 * h)))
            value = cavity(cb, jnp.concatenate(tiles, axis=1))
            for h in range(2):
                main_ref[h, group * size : (group + 1) * size, :] = value[:, h * LANES : (h + 1) * LANES]
            inside = (lane >= 32 * group) & (lane < 32 * group + 24)
            rest_back = jnp.where(inside, turn(extra, 32 * group - at - 16), rest_back)
    rest = cavity(cb, rest_back)
    for group in range(groups):
        for st in range(GROUP):
            level = [rest[st * LEVELS + 32 * c : st * LEVELS + 32 * c + 32] for c in range(2)]
            value = jnp.where(short < 24, turn(level[0], -32 * group), 0.0)
            value = jnp.where((short >= 32) & (short < 56), turn(level[1], 32 - 32 * group), value)
            at = (group * GROUP + st) * 32
            rest_ref[at : at + 32, :] = value

    for first in range(0, STATES, 4):
        for second in range(0, first + 4, 4):

            def add(tile, sums, load):
                a = [load(first + n, tile) for n in range(4)]
                b = a if first == second else [load(second + n, tile) for n in range(4)]
                return tuple(sums[p * 4 + q] + a[p] * b[q] for p in range(4) for q in range(4))

            sums = (jnp.zeros((8, LANES), F32),) * 16
            for tile in range(8):
                for h in range(2):
                    sums = add(tile, sums, lambda st, n: main_ref[h, st * LEVELS + n * 8 : st * LEVELS + n * 8 + 8, :])
            for tile in range(4):
                sums = add(tile, sums, lambda st, n: rest_ref[st * 32 + n * 8 : st * 32 + n * 8 + 8, :])
            for p in range(4):
                for q in range(4):
                    total = jnp.sum(sums[p * 4 + q], axis=0, keepdims=True)
                    at = flat_place(first + p, second + q)
                    rows_ref[at : at + 1, :] = total
                    if first != second:
                        at = flat_place(second + q, first + p)
                        rows_ref[at : at + 1, :] = total
    flat = lax.dot_general(
        jnp.ones((32, LANES), F32), rows_ref[...], (((1,), (1,)), ((), ())), precision=HIGHEST,
        preferred_element_type=F32,
    )
    for h in range(2):
        gram_ref[pl.ds(h, 32, stride=2), :] = flat[:, h * LANES : (h + 1) * LANES]


def mix_kernel(scale, gram_ref, main_ref, rest_ref, send_ref, coef_ref):
    gram = gram_ref[0:2, :]
    for z in range(1, 8):
        gram = gram + gram_ref[2 * z : 2 * z + 2, :]
    gram = gram * scale
    square = [
        pltpu.roll(jnp.broadcast_to(gram[h : h + 1], (8, LANES)), 0, 1, stride=16, stride_axis=0)
        for h in range(2)
    ]
    row, col = iota((STATES, LANES), 0), iota((STATES, LANES), 1)
    work = jnp.where(col < STATES, jnp.concatenate(square, axis=0), (col == row + STATES).astype(F32))
    def lanes(value, j):
        return jnp.broadcast_to(value[:, j : j + 1], (value.shape[0], LANES))

    for j in range(0, STATES, 2):
        first, second = work[j : j + 1, :], work[j + 1 : j + 2, :]
        left, right = lanes(work, j), lanes(work, j + 1)
        side = lanes(first, j + 1)
        over = 1.0 / lanes(first, j)
        factor = side * over
        below = 1.0 / (lanes(second, j + 1) - side * factor)
        second = (second - factor * first) * below
        right = right - left * factor
        work = work - jnp.where(row > j, left, 0.0) * (first * over) - jnp.where(row > j + 1, right, 0.0) * second
    diagonal = jnp.sum(jnp.where(col == row, work, 0.0), axis=1, keepdims=True)
    inverse = work / jnp.sqrt(diagonal)
    for st in range(STATES):
        column = jnp.broadcast_to(inverse[:, STATES + st : STATES + st + 1], (STATES, LANES))
        coef_ref[st * STATES : (st + 1) * STATES, :] = column

    lane = iota((8, LANES), 1)

    def mixed(loads):
        values = [[load(st) for load in loads] for st in range(STATES)]
        for t in range(STATES):
            sums = [None] * len(loads)
            for st in range(t + 1):
                factor = coef_ref[st * STATES + t : st * STATES + t + 1, :]
                for n in range(len(loads)):
                    term = factor * values[st][n]
                    sums[n] = term if sums[n] is None else sums[n] + term
            yield t, sums

    def tile(n, carry):
        start = pl.multiple_of(n * 8, 8)
        for c in range(2):
            loads = [
                lambda st, h=h: main_ref[h, pl.ds(st * LEVELS + c * 32 + start, 8), :] for h in range(2)
            ]
            for t, sums in mixed(loads):
                z, s = t // 2, t % 2
                for h in range(2):
                    at = (z * 32 + start) * ROWS + h * 4 + s * 2 + c
                    send_ref[pl.ds(at, 8, stride=ROWS), :] = sums[h]
        loads = [lambda st: rest_ref[pl.ds(st * 32 + start, 8), :]]
        seventh = None
        for t, sums in mixed(loads):
            z, s = t // 2, t % 2
            if s == 0:
                seventh = sums[0]
            else:
                seventh = seventh + turn(sums[0], 64)
                send_ref[pl.ds((z * 32 + start) * ROWS + 8, 8, stride=ROWS), :] = seventh
        return carry

    lax.fori_loop(0, 4, tile, 0, unroll=2)


def tail_kernel(recv_ref, out_hbm, out_ref, chunks_ref, tiles_ref, sems):
    copies = []
    lane = iota((M, LANES), 1)
    lane8 = iota((8, LANES), 1)
    lane20 = iota((20, LANES), 1)
    for s in range(2):
        for c in range(2):
            e = s * 2 + c
            chunk_ref, tile_ref = chunks_ref.at[e], tiles_ref.at[e]
            for m in range(12):
                g, h = m // 2, m % 2
                chunk_ref[m] = recv_ref[pl.ds(g * M * ROWS + h * 4 + e, M, stride=ROWS), :]
            for h in range(2):
                chunk_ref[12, 16 * h : 16 * h + 16] = recv_ref[pl.ds(240 * ROWS + h * 4 + e, 16, stride=ROWS), :]
            extras = []
            for g in range(2):
                seventh = recv_ref[pl.ds(g * M * ROWS + 8, M, stride=ROWS), :]
                extra = jnp.where(
                    lane < 8, pltpu.roll(chunk_ref[2 * g], 8, 1), pltpu.roll(chunk_ref[2 * g + 1], 16, 1)
                )
                extras.append(jnp.where(lane < 16, extra, pltpu.roll(seventh, (16 - 32 * e) % LANES, 1)))
            first, second, third = (extras[1][8 * n : 8 * n + 8] for n in range(3))
            chunk_ref[12, 32:40] = jnp.where(
                lane8 < 40,
                first,
                jnp.where(lane8 < 80, pltpu.roll(second, 40, 1), pltpu.roll(third, 80, 1)),
            )
            chunk_ref[13] = extras[0]
            for v in range(13):
                low = pltpu.roll(chunk_ref[v], (LANES - 8 * v) % LANES, 1) if v else chunk_ref[v]
                high = pltpu.roll(chunk_ref[v + 1], 120 - 8 * v, 1)
                tile_ref[v] = jnp.where(lane < 120 - 8 * v, low, high)
            for u in range(25):
                if u < 12:
                    value = tile_ref[u, 0:20]
                elif u == 12:
                    value = jnp.where(lane20 < 64, tile_ref[12, 0:20], turn(tile_ref[0, 20:40], 64))
                else:
                    value = turn(jnp.where(lane20 < 64, tile_ref[u - 12, 20:40], tile_ref[u - 13, 20:40]), 64)
                out_ref[pl.ds(s * 1000 + u * 2 + c, 20, stride=50), :] = value
        part = pl.ds(s * 1000, 1000)
        copies.append(pltpu.make_async_copy(out_ref.at[part], out_hbm.at[part], sems.at[s]))
        copies[-1].start()
    for copy in copies:
        copy.wait()


def call(kernel, outs, scratch, cost, places="v", limit=SMALL_VMEM, out_place="v"):
    spaces = {"v": pltpu.VMEM, "h": pltpu.HBM}
    return pl.pallas_call(
        kernel,
        out_shape=outs,
        in_specs=[pl.BlockSpec(memory_space=spaces[p]) for p in places],
        out_specs=jax.tree.map(lambda _: pl.BlockSpec(memory_space=spaces[out_place]), outs),
        scratch_shapes=scratch,
        compiler_params=pltpu.CompilerParams(vmem_limit_bytes=limit),
        cost_estimate=pl.CostEstimate(flops=cost, bytes_accessed=1 << 20, transcendentals=0),
    )


def shape(*dims, dtype=F32):
    return jax.ShapeDtypeStruct(dims, dtype)


def exchange(blocks, axes):
    count = 1
    for a in axes:
        count *= lax.axis_size(a)
    rows = blocks.shape[0] // count
    value = blocks.reshape(count, 1, rows * LANES)
    value = lax.all_to_all(value, axes, split_axis=0, concat_axis=0, tiled=True)
    return value.reshape(blocks.shape)


def body(states, membrane_step, cavity_forward, coupling, membrane_forward, cavity_back, membrane_back):
    panel, levels, joint = states.shape
    everyone = ("state", "core", "plane")
    by_tile = Layout(major_to_minor=(0, 2, 1, 3))
    linear = with_layout_constraint(states.reshape(panel, levels, joint // LANES, LANES), by_tile)
    linear = jnp.swapaxes(linear, 1, 2).reshape(-1, LANES)
    blocks = shape(256 * ROWS, LANES)
    send = call(
        head_kernel,
        blocks,
        [
            pltpu.VMEM((256 * ROWS, LANES), F32),
            pltpu.VMEM((2208, LANES), F32),
            pltpu.VMEM((M, M), F32),
            pltpu.VMEM((4, 48, 14 * LANES), F32),
            pltpu.VMEM((4, M, 14 * LANES), F32),
            pltpu.SemaphoreType.DMA((10,)),
        ],
        1 << 20,
        "hh",
        LARGE_VMEM,
        "h",
    )(linear, membrane_step)
    wides = [shape(LEVELS, 4 * LEVELS, dtype=BF16)] * 2
    squares = [shape(2, LANES, LANES, dtype=BF16)] * 4
    operands = call(operands_kernel, (*wides, *squares, shape(2, LEVELS, LANES)), [], 1 << 27, "vvvvv")(
        cavity_forward, coupling, membrane_forward, cavity_back, membrane_back
    )
    recv = exchange(send, everyone)
    main, rest, gram = call(
        step_kernel,
        (shape(2, STATES * LEVELS, LANES), shape(STATES * 32, LANES), shape(64, LANES)),
        [pltpu.VMEM((STATES * STATES, LANES), F32)],
        1 << 30,
        "vvvvvvvv",
    )(recv, *operands)
    gram = lax.all_to_all(gram.reshape(32, 2, LANES), ("plane", "core"), split_axis=0, concat_axis=0, tiled=True)
    gram = jnp.broadcast_to(jnp.sum(gram, axis=0, keepdims=True), (8, 2, LANES))
    gram = lax.all_to_all(gram, "state", split_axis=0, concat_axis=0, tiled=True)
    scale = 1.0 / float(LEVELS * joint)
    send = call(
        lambda *refs: mix_kernel(scale, *refs),
        blocks,
        [pltpu.VMEM((STATES * STATES, LANES), F32)],
        1 << 27,
        "vvv",
    )(gram.reshape(16, LANES), main, rest)
    recv = exchange(send, everyone)
    out = call(
        tail_kernel,
        shape(2000, LANES),
        [
            pltpu.VMEM((2208, LANES), F32),
            pltpu.VMEM((4, 14, M, LANES), F32),
            pltpu.VMEM((4, 13, M, LANES), F32),
            pltpu.SemaphoreType.DMA((2,)),
        ],
        1 << 20,
        out_place="h",
    )(recv)
    out = out.reshape(panel, joint // LANES, levels, LANES)
    return with_layout_constraint(jnp.swapaxes(out, 1, 2), by_tile).reshape(panel, levels, joint)


def solution(mesh):
    states = mesh.shape["state"]
    cores = Mesh(mesh.devices.reshape(states, -1, 2), ("state", "plane", "core"))
    out_specs = P("state", ("plane", "core"), None)
    in_specs = (out_specs, P(), P(), P(), P(), P(), P())
    return jax.shard_map(body, mesh=cores, in_specs=in_specs, out_specs=out_specs, check_vma=False)
```
